512 devices in a mesh: freq: 8 (over y, core), pair: 64 (over x, z).
Axes of the slice: x: 4, y: 4, z: 16, core: 2. Of those that a mesh axis runs over, the one named last changes fastest.
Arguments:
- spectra: bfloat16 [2, 24, 512, 16384], P(None, 'freq', None, 'pair'), may hold values from -6 to 6
- pair_blocks: int32 [1024, 2], P('pair'), may hold values from 0 to 127, as said below
- pair_valid: int32 [1024], P('pair'), may hold values from 0 to 1, as said below
Outputs:
- stack: float32 [512, 16384], P('freq', 'pair')
The draws below stay inside these ranges and needn't reach their ends.
Inputs may be any that keep to these rules, and one draw needn't show every extreme that they name: `pair_blocks`: row r belongs to owner r // 16; its first block lies in [owner * 2, (owner + 1) * 2); its second block is at or after the first and at most 6 blocks after it, and this largest distance occurs in every draw. `pair_valid`: within each owner's 16 rows the ones come first; every owner has at least one, and some owner has all 16.
All inputs are finite; a program needn't handle non-finite values.
Results may differ from the reference program's by a relative error of at most 0.00082.
Values may be sent and summed in bfloat16 or wider, within the bound.
A program may use at most 64 MiB of HBM per device.

```python
import jax
import jax.numpy as jnp
from jax import lax

FREQ = 512
SB = 128
HALF = 64
BLK_DEV = 2
PAIRS_DEV = 16
DEPTH = 3
WIN = 24
NBLK = 128
STATIONS = 16384
PAIRS = 1024


def draw_pair_blocks(key, part):
    key = jax.random.fold_in(key, 11)
    first_key, reach_key = jax.random.split(key)
    owner = jnp.arange(PAIRS) // PAIRS_DEV
    slot_index = jnp.arange(PAIRS) % PAIRS_DEV
    first_block = owner * BLK_DEV + jax.random.randint(first_key, (PAIRS,), 0, BLK_DEV)
    reach = jax.random.randint(reach_key, (PAIRS,), 0, DEPTH * BLK_DEV + 1)
    leading = (owner == 0) & (slot_index == 0)
    trailing = (owner == NBLK // BLK_DEV - 1) & (slot_index == 0)
    first_block = jnp.where(leading, 0, first_block)
    reach = jnp.where(leading, DEPTH * BLK_DEV, reach)
    first_block = jnp.where(trailing, NBLK - 1, first_block)
    second_block = jnp.minimum(first_block + reach, NBLK - 1)
    return jnp.stack([first_block, second_block], axis=1).astype(jnp.int32)


def draw_pair_valid(key, part):
    key = jax.random.fold_in(key, 23)
    owners = NBLK // BLK_DEV
    drawn = jax.random.randint(key, (owners,), 0, PAIRS_DEV)
    counts = 1 + drawn * drawn // PAIRS_DEV
    counts = counts.at[0].set(PAIRS_DEV)
    owner = jnp.arange(PAIRS) // PAIRS_DEV
    slot_index = jnp.arange(PAIRS) % PAIRS_DEV
    return (slot_index < counts[owner]).astype(jnp.int32)


def levels(rng, extent, cuts, least, largest):
    level = 1.0
    for dim, parts in cuts:
        draws = jax.random.uniform(jax.random.fold_in(jax.random.fold_in(rng, 6), dim), (parts,), jnp.float32, least / len(cuts), largest / len(cuts))
        level = level * jnp.repeat(jnp.exp(draws), extent[dim] // parts).reshape((-1,) + (1,) * (len(extent) - 1 - dim))
    return level


def noise(key, extent, spread, limit, cuts=(), dtype=jnp.bfloat16):
    entries = spread * jax.random.normal(key, extent, jnp.float32)
    if cuts:
        entries = entries * levels(key, extent, cuts, -0.22, 0.18)
    return jnp.clip(entries, -limit, limit).astype(dtype)


def setup_inputs(seed: int = 0) -> dict:
    splits = jax.random.split(jax.random.key(seed), 4)
    spectra = noise(splits[0], (2, WIN, FREQ, STATIONS), 1.0, 6.0, ((1, 8), (3, 64)))
    pair_blocks = draw_pair_blocks(jax.random.fold_in(splits[3], 71), 0)
    pair_valid = draw_pair_valid(jax.random.fold_in(splits[3], 71), 0)
    return {"spectra": spectra, "pair_blocks": pair_blocks, "pair_valid": pair_valid}


EPS = 1e-06

def whiten(spectra):
    spectra_f32 = spectra.astype(jnp.float32)
    magnitude = jnp.sqrt(spectra_f32[0] * spectra_f32[0] + spectra_f32[1] * spectra_f32[1])
    freq_bins = jnp.arange(spectra_f32.shape[2])
    window = (jnp.abs(freq_bins[:, None] - freq_bins[None, :]) <= HALF).astype(jnp.float32)
    counted = lax.optimization_barrier(jnp.sum(window, axis=1))
    smooth = jnp.einsum('fg,wgs->wfs', window, magnitude, precision=lax.Precision.HIGHEST) / counted[None, :, None]
    return (spectra_f32 / (smooth + EPS)[None]).astype(jnp.bfloat16)

def coherence_sums(left_block, right_block, scale):
    win_count = left_block.shape[1]
    freq_count = left_block.shape[2]
    block_size = left_block.shape[3]
    stacked_left = left_block.reshape(2 * win_count, freq_count, block_size)
    stacked_right = jnp.stack([right_block.reshape(2 * win_count, freq_count, block_size), jnp.concatenate([-right_block[1], right_block[0]], axis=0)])
    product = jnp.einsum('kfi,pkfj->pfij', stacked_left, stacked_right, precision=lax.Precision.HIGHEST)
    modulus = jnp.sqrt(product[0] * product[0] + product[1] * product[1]) * scale
    return (lax.optimization_barrier(jnp.sum(modulus, axis=2)), lax.optimization_barrier(jnp.sum(modulus, axis=1)))

def add_block(totals, index, values):
    current = lax.dynamic_index_in_dim(totals, index, 1, keepdims=False)
    return lax.dynamic_update_index_in_dim(totals, current + values, index, 1)

def reference(spectra, pair_blocks, pair_valid):
    whitened = whiten(spectra)
    blocks = whitened.reshape(2, WIN, FREQ, NBLK, SB)
    scale = 1.0 / (WIN * SB)

    def visit(totals, item):
        pair_row, live_flag = item
        left_block = lax.dynamic_index_in_dim(blocks, pair_row[0], 3, keepdims=False).astype(jnp.float32)
        right_block = lax.dynamic_index_in_dim(blocks, pair_row[1], 3, keepdims=False).astype(jnp.float32)
        row_sums, col_sums = coherence_sums(left_block, right_block, scale)
        weight = live_flag.astype(jnp.float32)
        totals = add_block(totals, pair_row[0], weight * row_sums)
        totals = add_block(totals, pair_row[1], weight * col_sums)
        return (totals, None)
    start_totals = jnp.zeros((FREQ, NBLK, SB), jnp.float32)
    totals, unused = lax.scan(visit, start_totals, (pair_blocks, pair_valid))
    return totals.reshape(FREQ, NBLK * SB)
```

```python
import functools

import jax
import jax.numpy as jnp
from jax import lax
from jax.experimental import pallas as pl
from jax.experimental.pallas import tpu as pltpu
from jax.sharding import PartitionSpec as P

MESH = pl.DeviceIdType.MESH
SB = 128
HALF = 64
EPS = 1e-06
TINY = 1.1754944e-38
FQ = 8
OWN = 64
WIN = 24
W_DEV = 3
FREQ = 512
F_DEV = 64
ST = 256
T = 4
F_PART = F_DEV // T
F_HALF = F_PART // 2
KDIM = 2 * WIN
UNROLL = 4


def modulus(square):
    return square * lax.rsqrt(jnp.maximum(square, TINY))


def whiten(spec, white):
    @pl.loop(0, W_DEV)
    def _(w):
        re = spec[0, w].astype(jnp.float32)
        im = spec[1, w].astype(jnp.float32)
        mag = modulus(re * re + im * im)
        high = mag.astype(jnp.bfloat16)
        rest = mag - high.astype(jnp.float32)
        mid = rest.astype(jnp.bfloat16)
        low = (rest - mid.astype(jnp.float32)).astype(jnp.bfloat16)
        for tile in range(FREQ // 128):
            first = tile * 128
            start = min(max(first - HALF, 0), FREQ - 256)
            out_bin = lax.broadcasted_iota(jnp.int32, (128, 256), 0) + first
            in_bin = lax.broadcasted_iota(jnp.int32, (128, 256), 1) + start
            band = jnp.where(jnp.abs(out_bin - in_bin) <= HALF, 1.0, 0.0).astype(jnp.bfloat16)
            rows = slice(start, start + 256)
            total = jnp.dot(band, low[rows], preferred_element_type=jnp.float32)
            total += jnp.dot(band, mid[rows], preferred_element_type=jnp.float32)
            total += jnp.dot(band, high[rows], preferred_element_type=jnp.float32)
            bins = lax.broadcasted_iota(jnp.int32, (128, ST), 0) + first
            counted = jnp.minimum(bins + HALF, FREQ - 1) - jnp.maximum(bins - HALF, 0) + 1
            inverse = 1.0 / (total / counted.astype(jnp.float32) + EPS)
            here = slice(first, first + 128)
            white[0, w, here] = (re[here] * inverse).astype(jnp.bfloat16)
            white[1, w, here] = (im[here] * inverse).astype(jnp.bfloat16)


def one_bin(anchor, partners, weight, f):
    first = anchor[f]
    wide = first.astype(jnp.float32)
    turned = jnp.concatenate([wide[WIN:], -wide[:WIN]], axis=0).astype(jnp.bfloat16)
    left = jnp.concatenate([first, turned], axis=1).T
    right = [partner[f] for partner in partners]
    cols = [None] * 8
    rows = []
    for p in range(2):
        pieces = []
        for i in range(2):
            at = p * SB + i * 64
            lhs = jnp.concatenate([left[at : at + 64], left[ST + at : ST + at + 64]], axis=0)
            piece = None
            for s in range(4):
                cross = jnp.dot(lhs, right[s], preferred_element_type=jnp.float32)
                for h in range(2):
                    q = 2 * s + h
                    if not p <= q <= p + 6:
                        continue
                    lanes = slice(h * SB, (h + 1) * SB)
                    re, im = cross[:64, lanes], cross[64:, lanes]
                    value = modulus(re * re + im * im) * weight(p, q)
                    col = jnp.sum(value.reshape(8, 8, SB), axis=0)
                    cols[q] = col if cols[q] is None else cols[q] + col
                    piece = value if piece is None else piece + value
            pieces.append(piece)
        across = jnp.concatenate(pieces, axis=0).T
        rows.append(jnp.sum(across.reshape(16, 8, SB), axis=0).sum(axis=0, keepdims=True))
    return rows, [col.sum(axis=0, keepdims=True) for col in cols]


def eight_bins(anchor_slot, partners, weight, start, out):
    line = lax.broadcasted_iota(jnp.int32, (8, SB), 0)

    def step(k, tiles):
        rows, cols = one_bin(partners[anchor_slot], partners, weight, start + k)
        for p in range(2):
            cols[2 * anchor_slot + p] = cols[2 * anchor_slot + p] + rows[p]
        return tuple(jnp.where(line == k, cols[q], tiles[q]) for q in range(8))

    zero = jnp.zeros((8, SB), jnp.float32)
    tiles = lax.fori_loop(0, 8, step, (zero,) * 8, unroll=UNROLL)
    for q in range(8):
        out[q // 2, pl.ds(start, 8), (q % 2) * SB : (q % 2 + 1) * SB] = tiles[q]


def kernel(
    spec, blocks, valid, out,
    white, landed, wide, held, left, right, far, counts, sums, back,
    a2a_send, a2a_recv, hop_send, hop_recv, far_send, far_recv,
    cnt_send, cnt_recv, ret_send, ret_recv,
):
    me = lax.axis_index("freq")
    owner = lax.axis_index("pair")

    def along(by):
        return (me, lax.rem(owner + by + OWN, OWN))

    barrier = pltpu.get_barrier_semaphore()
    for by in range(1, FQ):
        pl.semaphore_signal(barrier, 1, device_id=(lax.rem(me + by, FQ), owner), device_id_type=MESH)
    for by in (-2, -1, 1, 2):
        pl.semaphore_signal(barrier, 1, device_id=along(by), device_id_type=MESH)

    row = lax.broadcasted_iota(jnp.int32, (16, SB), 0)
    table = jnp.zeros((16, SB), jnp.float32)
    for slot in range(16):
        first = blocks[slot, 0] - 2 * owner
        second = blocks[slot, 1] - 2 * owner
        table += jnp.where(row == first * 8 + second, valid[slot].astype(jnp.float32), 0.0)
    counts[2] = table * (1.0 / (WIN * SB))

    whiten(spec, white)
    mine = pl.multiple_of(me * F_DEV, F_DEV)
    landed[me] = white[:, :, pl.ds(mine, F_DEV), :]
    pl.semaphore_wait(barrier, FQ - 1 + 4)

    def copy(src, dst, send, recv, device):
        return pltpu.make_async_remote_copy(
            src_ref=src, dst_ref=dst, send_sem=send, recv_sem=recv, device_id=device, device_id_type=MESH
        )

    def regroup(by, t):
        peer = lax.rem(me + by, FQ)
        bins = pl.ds(pl.multiple_of(peer * F_DEV + t * F_PART, F_PART), F_PART)
        return copy(
            white.at[:, :, bins, :],
            landed.at[me, :, :, pl.ds(pl.multiple_of(t * F_PART, F_PART), F_PART), :],
            a2a_send.at[by - 1, t], a2a_recv.at[by - 1, t], (peer, owner),
        )

    def count_copies():
        return [
            copy(counts.at[2], counts.at[to], cnt_send.at[i], cnt_recv.at[i], along(by))
            for i, (to, by) in enumerate(((1, 1), (0, 2), (3, -1)))
        ]

    def hop(side, t, part):
        bins = pl.ds(t * F_PART + part * F_HALF, F_HALF)
        dst, by = ((right, -1), (left, 1))[side]
        at = 2 * t + part
        return copy(held.at[bins], dst.at[bins], hop_send.at[side, at], hop_recv.at[side, at], along(by))

    def relay(part, t):
        bins = pl.ds(t * F_PART + part * F_HALF, F_HALF)
        src, by = ((right, -1), (left, 1))[part]
        at = 2 * t + part
        return copy(src.at[bins], far.at[bins], far_send.at[at], far_recv.at[at], along(by))

    def returned(part, t):
        at = 2 * t + part
        bins = pl.ds(pl.multiple_of(at * F_HALF, F_HALF), F_HALF)
        plan = (((0, -1, 0), (2, 1, 1), (3, 2, 2)), ((1, -1, 0), (3, 1, 1), (0, -2, 2)))[part]
        return [
            copy(sums.at[slot, bins, :], back.at[to, bins, :], ret_send.at[to, at], ret_recv.at[to, at], along(by))
            for slot, by, to in plan
        ]

    def arrange(t):
        for by in range(1, FQ):
            regroup(by, t).wait_recv()
        bins = pl.ds(pl.multiple_of(t * F_PART, F_PART), F_PART)
        for source in range(FQ):
            for c in range(2):
                for w in range(W_DEV):
                    k = c * WIN + source * W_DEV + w
                    value = landed[source, c, w, bins, :].astype(jnp.float32)
                    for h in range(2):
                        wide[h, k * F_PART : (k + 1) * F_PART, :] = value[:, h * SB : (h + 1) * SB]
        for f in range(F_PART):
            for h in range(2):
                value = wide[h, pl.ds(f, KDIM, stride=F_PART), :]
                held[t * F_PART + f, :, h * SB : (h + 1) * SB] = value.astype(jnp.bfloat16)
        for side, part in ((0, 0), (1, 1), (0, 1), (1, 0)):
            hop(side, t, part).start()

    def pass_on(t):
        hop(0, t, 0).wait_recv()
        relay(0, t).start()
        hop(1, t, 1).wait_recv()
        relay(1, t).start()

    def compute(t):
        hop(1, t, 0).wait_recv()
        relay(0, t).wait_recv()
        start = pl.multiple_of(t * F_PART, F_HALF)
        eight_bins(0, (left, held, right, far), lambda p, q: counts[1, p * 8 + q : p * 8 + q + 1, :], start, sums)
        for item in returned(0, t):
            item.start()
        hop(0, t, 1).wait_recv()
        relay(1, t).wait_recv()
        start = pl.multiple_of(t * F_PART + F_HALF, F_HALF)

        def weight(p, q):
            at = (q % 2) * 8 + 6 - 2 * (q // 2) + p
            return counts[q // 2, at : at + 1, :]

        eight_bins(3, (far, left, held, right), weight, start, sums)
        for item in returned(1, t):
            item.start()

    for t in range(T):
        for by in range(1, FQ):
            regroup(by, t).start()
    for item in count_copies():
        item.start()
    arrange(0)
    for item in count_copies():
        item.wait_recv()

    @pl.loop(0, T + 1)
    def _(t):
        @pl.when(t < T - 1)
        def _():
            arrange(t + 1)

        @pl.when(t < T)
        def _():
            pass_on(t)

        @pl.when(t > 0)
        def _():
            compute(t - 1)

    for t in range(T):
        for part in range(2):
            for item in returned(part, t):
                item.wait_recv()
            bins = slice((2 * t + part) * F_HALF, (2 * t + part + 1) * F_HALF)
            out[bins] = (sums[1 + part, bins] + back[0, bins]) + (back[1, bins] + back[2, bins])
    for t in range(T):
        for by in range(1, FQ):
            regroup(by, t).wait_send()
        for part in range(2):
            for side in range(2):
                hop(side, t, part).wait_send()
            relay(part, t).wait_send()
            for item in returned(part, t):
                item.wait_send()
    for item in count_copies():
        item.wait_send()


def body(spectra, pair_blocks, pair_valid):
    dma = pltpu.SemaphoreType.DMA
    band = pltpu.VMEM((F_DEV, KDIM, ST), jnp.bfloat16)
    vmem = pl.BlockSpec(memory_space=pltpu.VMEM)
    smem = pl.BlockSpec(memory_space=pltpu.SMEM)
    return pl.pallas_call(
        kernel,
        out_shape=jax.ShapeDtypeStruct((F_DEV, ST), jnp.float32),
        in_specs=[vmem, smem, smem],
        out_specs=vmem,
        scratch_shapes=[
            pltpu.VMEM((2, W_DEV, FREQ, ST), jnp.bfloat16),
            pltpu.VMEM((FQ, 2, W_DEV, F_DEV, ST), jnp.bfloat16),
            pltpu.VMEM((2, KDIM * F_PART, SB), jnp.float32),
            band, band, band, band,
            pltpu.VMEM((4, 16, SB), jnp.float32),
            pltpu.VMEM((4, F_DEV, ST), jnp.float32),
            pltpu.VMEM((3, F_DEV, ST), jnp.float32),
            dma((FQ - 1, T)), dma((FQ - 1, T)),
            dma((2, 2 * T)), dma((2, 2 * T)),
            dma((2 * T,)), dma((2 * T,)),
            dma((3,)), dma((3,)),
            dma((3, 2 * T)), dma((3, 2 * T)),
        ],
        compiler_params=pltpu.CompilerParams(
            collective_id=0, has_side_effects=True, vmem_limit_bytes=40 * 2**20
        ),
        cost_estimate=pl.CostEstimate(flops=8 * 10**9, bytes_accessed=2 * 2**20, transcendentals=0),
    )(spectra, pair_blocks, pair_valid)


def solution(mesh):
    in_specs = (P(None, "freq", None, "pair"), P("pair", None), P("pair"))
    out_specs = P("freq", "pair")
    return jax.shard_map(body, mesh=mesh, in_specs=in_specs, out_specs=out_specs, check_vma=False)
```

```python
import functools

import jax
import jax.numpy as jnp
from jax import lax
from jax.experimental import pallas as pl
from jax.experimental.pallas import tpu as pltpu
from jax.sharding import PartitionSpec as P

MESH = pl.DeviceIdType.MESH
SB = 128
HALF = 64
EPS = 1e-06
TINY = 1.1754944e-38
FQ = 8
OWN = 64
WIN = 24
W_DEV = 3
FREQ = 512
F_DEV = 64
ST = 256
T = 4
F_PART = F_DEV // T
F_HALF = F_PART // 2
KDIM = 2 * WIN
UNROLL = 4
LAST = (0, 0, 1, 1, 0, 1, 0, 1)


def modulus(square):
    return square * lax.rsqrt(jnp.maximum(square, TINY))


def whiten(spec, white, first_window, windows):
    @pl.loop(first_window, first_window + windows)
    def _(w):
        re = spec[0, w].astype(jnp.float32)
        im = spec[1, w].astype(jnp.float32)
        mag = modulus(re * re + im * im)
        high = mag.astype(jnp.bfloat16)
        rest = mag - high.astype(jnp.float32)
        mid = rest.astype(jnp.bfloat16)
        low = (rest - mid.astype(jnp.float32)).astype(jnp.bfloat16)
        for tile in range(FREQ // 128):
            first = tile * 128
            start = min(max(first - HALF, 0), FREQ - 256)
            out_bin = lax.broadcasted_iota(jnp.int32, (128, 256), 0) + first
            in_bin = lax.broadcasted_iota(jnp.int32, (128, 256), 1) + start
            band = jnp.where(jnp.abs(out_bin - in_bin) <= HALF, 1.0, 0.0).astype(jnp.bfloat16)
            rows = slice(start, start + 256)
            total = jnp.dot(band, low[rows], preferred_element_type=jnp.float32)
            total += jnp.dot(band, mid[rows], preferred_element_type=jnp.float32)
            total += jnp.dot(band, high[rows], preferred_element_type=jnp.float32)
            bins = lax.broadcasted_iota(jnp.int32, (128, ST), 0) + first
            counted = jnp.minimum(bins + HALF, FREQ - 1) - jnp.maximum(bins - HALF, 0) + 1
            inverse = 1.0 / (total / counted.astype(jnp.float32) + EPS)
            here = slice(first, first + 128)
            two = slice(first // F_DEV, first // F_DEV + 2)
            white[0, w, two] = (re[here] * inverse).astype(jnp.bfloat16).reshape(2, F_DEV, ST)
            white[1, w, two] = (im[here] * inverse).astype(jnp.bfloat16).reshape(2, F_DEV, ST)


def one_bin(anchor, partners, weight, f):
    first = anchor[f]
    wide = first.astype(jnp.float32)
    turned = jnp.concatenate([wide[WIN:], -wide[:WIN]], axis=0).astype(jnp.bfloat16)
    left = jnp.concatenate([first, turned], axis=1).T
    right = {s: partner[f] for s, partner in partners.items()}
    cols = {}
    rows = []
    for p in range(2):
        pieces = []
        for i in range(2):
            at = p * SB + i * 64
            lhs = jnp.concatenate([left[at : at + 64], left[ST + at : ST + at + 64]], axis=0)
            piece = None
            for s in partners:
                cross = jnp.dot(lhs, right[s], preferred_element_type=jnp.float32)
                for h in range(2):
                    q = 2 * s + h
                    if not p <= q <= p + 6:
                        continue
                    lanes = slice(h * SB, (h + 1) * SB)
                    re, im = cross[:64, lanes], cross[64:, lanes]
                    value = modulus(re * re + im * im) * weight(p, q)
                    col = jnp.sum(value.reshape(8, 8, SB), axis=0)
                    cols[q] = cols[q] + col if q in cols else col
                    piece = value if piece is None else piece + value
            pieces.append(piece)
        across = jnp.concatenate(pieces, axis=0).T
        rows.append(jnp.sum(across.reshape(16, 8, SB), axis=0).sum(axis=0, keepdims=True))
    return rows, {q: col.sum(axis=0, keepdims=True) for q, col in cols.items()}


def eight_bins(anchor_slot, anchor, partners, weight, start, out):
    line = lax.broadcasted_iota(jnp.int32, (8, SB), 0)
    near = anchor_slot in partners
    own = [2 * anchor_slot, 2 * anchor_slot + 1]
    keys = sorted({2 * s + h for s in partners for h in range(2)} | set(own))

    def step(k, tiles):
        rows, cols = one_bin(anchor, partners, weight, start + k)
        for p in range(2):
            cols[own[p]] = cols[own[p]] + rows[p] if near else rows[p]
        return tuple(jnp.where(line == k, cols[q], tile) for q, tile in zip(keys, tiles))

    zero = jnp.zeros((8, SB), jnp.float32)
    tiles = lax.fori_loop(0, 8, step, (zero,) * len(keys), unroll=UNROLL)
    for q, tile in zip(keys, tiles):
        place = (q // 2, pl.ds(start, 8), slice((q % 2) * SB, (q % 2 + 1) * SB))
        out[place] = tile if near or q not in own else out[place] + tile


def kernel(
    spec_hbm, blocks_hbm, valid_hbm, out,
    spec, blocks, valid, load_sem, white, from_left, from_right, from_far, landed, more, wide,
    held, left, right, far, counts, sums, back,
    a2a_send, a2a_recv, more_send, more_recv, hop_send, hop_recv, far_send, far_recv,
    cnt_send, cnt_recv, ret_send, ret_recv, early_send, early_recv, ready,
):
    me = lax.axis_index("freq")
    owner = lax.axis_index("pair")

    def along(by):
        return (me, lax.rem(owner + by + OWN, OWN))

    def signal(sem, device):
        pl.semaphore_signal(sem, 1, device_id=device, device_id_type=MESH)

    barrier = pltpu.get_barrier_semaphore()
    for by in (-1, 1):
        signal(barrier, along(by))
    for by in range(1, FQ):
        signal(barrier, (lax.rem(me + by, FQ), owner))

    loads = [pltpu.make_async_copy(spec_hbm.at[:, w], spec.at[:, w], load_sem.at[w]) for w in range(W_DEV)]
    loads.append(pltpu.make_async_copy(blocks_hbm, blocks, load_sem.at[W_DEV]))
    loads.append(pltpu.make_async_copy(valid_hbm, valid, load_sem.at[W_DEV + 1]))
    for load in loads:
        load.start()
    loads[W_DEV].wait()
    loads[W_DEV + 1].wait()
    row = lax.broadcasted_iota(jnp.int32, (16, 16), 0)
    place = (blocks[0:1, :] - 2 * owner) * 8 + (blocks[1:2, :] - 2 * owner)
    table = jnp.sum(jnp.where(row == place, valid[...].astype(jnp.float32), 0.0), axis=1, keepdims=True)
    counts[2] = jnp.broadcast_to(table * (1.0 / (WIN * SB)), (16, SB))

    def copy(src, dst, send, recv, device):
        return pltpu.make_async_remote_copy(
            src_ref=src, dst_ref=dst, send_sem=send, recv_sem=recv, device_id=device, device_id_type=MESH
        )

    def early(side, w):
        dst, by = ((from_right, -1), (from_left, 1))[side]
        return copy(
            white.at[:, w, :, pl.ds(0, F_PART), :], dst.at[:, w],
            early_send.at[side, w], early_recv.at[side, w], along(by),
        )

    def early_relay(w):
        return copy(
            from_right.at[:, w], from_far.at[:, w], early_send.at[2, w], early_recv.at[2, w], along(-1)
        )

    def regroup_more(i, by):
        peer = lax.rem(me + by, FQ)
        src = (from_left, from_right, from_far)[i]
        return copy(
            src.at[:, :, peer, :, :], more.at[i, by - 1],
            more_send.at[i, by - 1], more_recv.at[i, by - 1], (peer, owner),
        )

    def part_bins(t):
        return pl.ds(pl.multiple_of(t * F_PART, F_PART), F_PART)

    def regroup(by, t):
        peer = lax.rem(me + by, FQ)
        return copy(
            white.at[:, :, peer, part_bins(t), :], landed.at[by - 1, :, :, part_bins(t), :],
            a2a_send.at[by - 1, t], a2a_recv.at[by - 1, t], (peer, owner),
        )

    def count_copies():
        return [
            copy(counts.at[2], counts.at[to], cnt_send.at[i], cnt_recv.at[i], along(by))
            for i, (to, by) in enumerate(((1, 1), (3, -1), (0, 2)))
        ]

    def hop(side, t, part):
        bins = pl.ds(t * F_PART + part * F_HALF, F_HALF)
        dst, by = ((right, -1), (left, 1))[side]
        at = 2 * t + part
        return copy(held.at[bins], dst.at[bins], hop_send.at[side, at], hop_recv.at[side, at], along(by))

    def relay(last, t, part):
        bins = pl.ds(t * F_PART + part * F_HALF, F_HALF)
        src, by = ((right, -1), (left, 1))[last]
        at = 2 * t + part
        return copy(src.at[bins], far.at[bins], far_send.at[at], far_recv.at[at], along(by))

    def returned(last, at, stage):
        bins = pl.ds(pl.multiple_of(at * F_HALF, F_HALF), F_HALF)
        plan = ((((2, 1, 1),), ((0, -1, 0), (3, 2, 2))), (((1, -1, 0),), ((3, 1, 1), (0, -2, 2))))[last][stage]
        return [
            copy(sums.at[slot, bins, :], back.at[to, bins, :], ret_send.at[to, at], ret_recv.at[to, at], along(by))
            for slot, by, to in plan
        ]

    def place_part(dst, t, first, others, arrived):
        for by in range(FQ):
            if by:
                arrived(by)
            for c in range(2):
                for w in range(W_DEV):
                    k = c * WIN + by * W_DEV + w
                    value = (others(by, c, w) if by else first(c, w)).astype(jnp.float32)
                    for h in range(2):
                        wide[h, k * F_PART : (k + 1) * F_PART, :] = value[:, h * SB : (h + 1) * SB]
        for f in range(F_PART):
            for h in range(2):
                value = wide[h, pl.ds(f, KDIM, stride=F_PART), :]
                dst[t * F_PART + f, :, h * SB : (h + 1) * SB] = value.astype(jnp.bfloat16)

    def arrange(t):
        bins = part_bins(t)
        place_part(
            held, t, lambda c, w: white[c, w, me, bins, :], lambda by, c, w: landed[by - 1, c, w, bins, :],
            lambda by: regroup(by, t).wait_recv(),
        )

    def arrange_more(i):
        src = (from_left, from_right, from_far)[i]
        place_part(
            (left, right, far)[i], 0, lambda c, w: src[c, w, me], lambda by, c, w: more[i, by - 1, c, w],
            lambda by: regroup_more(i, by).wait_recv(),
        )

    def start_hops(t):
        for side, part in ((0, 0), (1, 1), (0, 1), (1, 0)):
            hop(side, t, part).start()

    def pass_on(t):
        hop(0, t, 0).wait_recv()
        relay(0, t, 0).start()
        hop(1, t, 1).wait_recv()
        relay(1, t, 1).start()

    def weight_first(p, q):
        return counts[1, p * 8 + q : p * 8 + q + 1, :]

    def weight_last(p, q):
        at = (q % 2) * 8 + 6 - 2 * (q // 2) + p
        return counts[q // 2, at : at + 1, :]

    def compute(last, at, stage):
        start = pl.multiple_of(at * F_HALF, F_HALF)
        if last:
            partners = {0: far} if stage else {1: left, 2: held, 3: right}
            eight_bins(3, right, partners, weight_last, start, sums)
        else:
            partners = {3: far} if stage else {0: left, 1: held, 2: right}
            eight_bins(0, left, partners, weight_first, start, sums)
        for item in returned(last, at, stage):
            item.start()

    for w in range(W_DEV):
        loads[w].wait()
        whiten(spec, white, w, 1)
        if w == 0:
            pl.semaphore_wait(barrier, FQ - 1 + 2)
            signal(ready.at[0], along(1))
            signal(ready.at[1], along(-1))
        early(0, w).start()
        early(1, w).start()
    for t in (1, 2, 3, 0):
        for by in range(1, FQ):
            regroup(by, t).start()
    for item in count_copies()[:2]:
        item.start()
    arrange(1)
    start_hops(1)
    for w in range(W_DEV):
        early(0, w).wait_recv()
        early(1, w).wait_recv()
    for i in range(2):
        for by in range(1, FQ):
            regroup_more(i, by).start()
    pl.semaphore_wait(ready.at[0], 1)
    pl.semaphore_wait(ready.at[1], 1)
    count_copies()[2].start()

    @pl.loop(2, T)
    def _(t):
        arrange(t)
        start_hops(t)

    for w in range(W_DEV):
        early_relay(w).start()
    for part in range(2):
        hop(1, 1, part).wait_recv()
        relay(1, 1, part).start()
    for item in count_copies():
        item.wait_recv()
    hop(0, 1, 0).wait_recv()
    hop(0, 1, 1).wait_recv()

    @pl.loop(2, 4)
    def _(at):
        compute(1, at, 0)

    arrange(0)
    arrange_more(0)
    arrange_more(1)

    @pl.loop(0, 2)
    def _(at):
        compute(0, at, 0)

    @pl.loop(2, T)
    def _(t):
        pass_on(t)
        hop(1, t, 0).wait_recv()
        hop(0, t, 1).wait_recv()
        compute(0, 2 * t, 0)
        compute(1, 2 * t + 1, 0)

    for w in range(W_DEV):
        early_relay(w).wait_recv()
    for by in range(1, FQ):
        regroup_more(2, by).start()

    @pl.loop(2, 4)
    def _(at):
        relay(1, 1, at - 2).wait_recv()
        compute(1, at, 1)

    @pl.loop(2, T)
    def _(t):
        relay(0, t, 0).wait_recv()
        compute(0, 2 * t, 1)
        relay(1, t, 1).wait_recv()
        compute(1, 2 * t + 1, 1)

        @pl.when(t == 2)
        def _():
            arrange_more(2)

            @pl.loop(0, 2)
            def _(at):
                compute(0, at, 1)

    for at in range(2 * T):
        last = LAST[at]
        for item in returned(last, at, 0) + returned(last, at, 1):
            item.wait_recv()
        bins = slice(at * F_HALF, (at + 1) * F_HALF)
        out[bins] = (sums[1 + last, bins] + back[0, bins]) + (back[1, bins] + back[2, bins])
    for t in range(T):
        for by in range(1, FQ):
            regroup(by, t).wait_send()
        for part in range(2):
            at = 2 * t + part
            last = LAST[at]
            if t:
                hop(0, t, part).wait_send()
                hop(1, t, part).wait_send()
                relay(last, t, part).wait_send()
            for item in returned(last, at, 0) + returned(last, at, 1):
                item.wait_send()
    for w in range(W_DEV):
        early(0, w).wait_send()
        early(1, w).wait_send()
        early_relay(w).wait_send()
    for i in range(3):
        for by in range(1, FQ):
            regroup_more(i, by).wait_send()
    for item in count_copies():
        item.wait_send()


def body(spectra, pair_blocks, pair_valid):
    dma = pltpu.SemaphoreType.DMA
    band = pltpu.VMEM((F_DEV, KDIM, ST), jnp.bfloat16)
    early = pltpu.VMEM((2, W_DEV, FQ, F_PART, ST), jnp.bfloat16)
    vmem = pl.BlockSpec(memory_space=pltpu.VMEM)
    anywhere = pl.BlockSpec(memory_space=pl.ANY)
    return pl.pallas_call(
        kernel,
        out_shape=jax.ShapeDtypeStruct((F_DEV, ST), jnp.float32),
        in_specs=[anywhere, anywhere, anywhere],
        out_specs=vmem,
        scratch_shapes=[
            pltpu.VMEM((2, W_DEV, FREQ, ST), jnp.bfloat16),
            pltpu.VMEM((2, 16), jnp.int32),
            pltpu.VMEM((1, 16), jnp.int32),
            dma((W_DEV + 2,)),
            pltpu.VMEM((2, W_DEV, FQ, F_DEV, ST), jnp.bfloat16),
            early, early, early,
            pltpu.VMEM((FQ - 1, 2, W_DEV, F_DEV, ST), jnp.bfloat16),
            pltpu.VMEM((3, FQ - 1, 2, W_DEV, F_PART, ST), jnp.bfloat16),
            pltpu.VMEM((2, KDIM * F_PART, SB), jnp.float32),
            band, band, band, band,
            pltpu.VMEM((4, 16, SB), jnp.float32),
            pltpu.VMEM((4, F_DEV, ST), jnp.float32),
            pltpu.VMEM((3, F_DEV, ST), jnp.float32),
            dma((FQ - 1, T)), dma((FQ - 1, T)),
            dma((3, FQ - 1)), dma((3, FQ - 1)),
            dma((2, 2 * T)), dma((2, 2 * T)),
            dma((2 * T,)), dma((2 * T,)),
            dma((3,)), dma((3,)),
            dma((3, 2 * T)), dma((3, 2 * T)),
            dma((3, W_DEV)), dma((3, W_DEV)),
            pltpu.SemaphoreType.REGULAR((2,)),
        ],
        compiler_params=pltpu.CompilerParams(
            collective_id=0, has_side_effects=True, vmem_limit_bytes=60 * 2**20
        ),
        cost_estimate=pl.CostEstimate(flops=8 * 10**9, bytes_accessed=2 * 2**20, transcendentals=0),
    )(spectra, pair_blocks.T, pair_valid.reshape(1, 16))


def solution(mesh):
    in_specs = (P(None, "freq", None, "pair"), P("pair", None), P("pair"))
    out_specs = P("freq", "pair")
    return jax.shard_map(body, mesh=mesh, in_specs=in_specs, out_specs=out_specs, check_vma=False)
```

```python
import functools

import jax
import jax.numpy as jnp
from jax import lax
from jax.experimental import pallas as pl
from jax.experimental.pallas import tpu as pltpu
from jax.sharding import PartitionSpec as P

MESH = pl.DeviceIdType.MESH
SB = 128
HALF = 64
EPS = 1e-06
TINY = 1.1754944e-38
FQ = 8
OWN = 64
WIN = 24
W_DEV = 3
FREQ = 512
F_DEV = 64
ST = 256
T = 4
F_PART = F_DEV // T
F_HALF = F_PART // 2
KDIM = 2 * WIN
UNROLL = 4
LAST = (0, 0, 1, 1, 0, 1, 0, 1)


def modulus(square):
    return square * lax.rsqrt(jnp.maximum(square, TINY))


def whiten(spec, white, first_window, windows):
    @pl.loop(first_window, first_window + windows)
    def _(w):
        re = spec[0, w].astype(jnp.float32)
        im = spec[1, w].astype(jnp.float32)
        mag = modulus(re * re + im * im)
        high = mag.astype(jnp.bfloat16)
        rest = mag - high.astype(jnp.float32)
        mid = rest.astype(jnp.bfloat16)
        low = (rest - mid.astype(jnp.float32)).astype(jnp.bfloat16)
        for tile in range(FREQ // 128):
            first = tile * 128
            start = min(max(first - HALF, 0), FREQ - 256)
            out_bin = lax.broadcasted_iota(jnp.int32, (128, 256), 0) + first
            in_bin = lax.broadcasted_iota(jnp.int32, (128, 256), 1) + start
            band = jnp.where(jnp.abs(out_bin - in_bin) <= HALF, 1.0, 0.0).astype(jnp.bfloat16)
            rows = slice(start, start + 256)
            total = jnp.dot(band, low[rows], preferred_element_type=jnp.float32)
            total += jnp.dot(band, mid[rows], preferred_element_type=jnp.float32)
            total += jnp.dot(band, high[rows], preferred_element_type=jnp.float32)
            bins = lax.broadcasted_iota(jnp.int32, (128, ST), 0) + first
            counted = jnp.minimum(bins + HALF, FREQ - 1) - jnp.maximum(bins - HALF, 0) + 1
            inverse = 1.0 / (total / counted.astype(jnp.float32) + EPS)
            here = slice(first, first + 128)
            two = slice(first // F_DEV, first // F_DEV + 2)
            white[0, w, two] = (re[here] * inverse).astype(jnp.bfloat16).reshape(2, F_DEV, ST)
            white[1, w, two] = (im[here] * inverse).astype(jnp.bfloat16).reshape(2, F_DEV, ST)


def one_bin(anchor, partners, weight, f):
    first = anchor[f]
    wide = first.astype(jnp.float32)
    turned = jnp.concatenate([wide[WIN:], -wide[:WIN]], axis=0).astype(jnp.bfloat16)
    left = jnp.concatenate([first, turned], axis=1).T
    right = {s: partner[f] for s, partner in partners.items()}
    cols = {}
    rows = []
    for p in range(2):
        pieces = []
        for i in range(2):
            at = p * SB + i * 64
            lhs = jnp.concatenate([left[at : at + 64], left[ST + at : ST + at + 64]], axis=0)
            piece = None
            for s in partners:
                cross = jnp.dot(lhs, right[s], preferred_element_type=jnp.float32)
                for h in range(2):
                    q = 2 * s + h
                    if not p <= q <= p + 6:
                        continue
                    lanes = slice(h * SB, (h + 1) * SB)
                    re, im = cross[:64, lanes], cross[64:, lanes]
                    value = modulus(re * re + im * im) * weight(p, q)
                    col = jnp.sum(value.reshape(8, 8, SB), axis=0)
                    cols[q] = cols[q] + col if q in cols else col
                    piece = value if piece is None else piece + value
            pieces.append(piece)
        across = jnp.concatenate(pieces, axis=0).T
        rows.append(jnp.sum(across.reshape(16, 8, SB), axis=0).sum(axis=0, keepdims=True))
    return rows, {q: col.sum(axis=0, keepdims=True) for q, col in cols.items()}


def eight_bins(anchor_slot, anchor, partners, weight, start, out):
    line = lax.broadcasted_iota(jnp.int32, (8, SB), 0)
    near = anchor_slot in partners
    own = [2 * anchor_slot, 2 * anchor_slot + 1]
    keys = sorted({2 * s + h for s in partners for h in range(2)} | set(own))

    def step(k, tiles):
        rows, cols = one_bin(anchor, partners, weight, start + k)
        for p in range(2):
            cols[own[p]] = cols[own[p]] + rows[p] if near else rows[p]
        return tuple(jnp.where(line == k, cols[q], tile) for q, tile in zip(keys, tiles))

    zero = jnp.zeros((8, SB), jnp.float32)
    tiles = lax.fori_loop(0, 8, step, (zero,) * len(keys), unroll=UNROLL if len(partners) > 1 else 8)
    for q, tile in zip(keys, tiles):
        place = (q // 2, pl.ds(start, 8), slice((q % 2) * SB, (q % 2 + 1) * SB))
        out[place] = tile if near or q not in own else out[place] + tile


class Guarded:
    def __init__(self, copy, sends, receives):
        self.copy, self.sends, self.receives = copy, sends, receives

    def start(self):
        @pl.when(self.sends)
        def _():
            self.copy.start()

    def wait_send(self):
        @pl.when(self.sends)
        def _():
            self.copy.wait_send()

    def wait_recv(self):
        @pl.when(self.receives)
        def _():
            self.copy.wait_recv()


def kernel(
    spec_hbm, blocks_hbm, valid_hbm, out,
    spec, blocks, valid, load_sem, white, from_left, from_right, from_far, landed, more, wide,
    held, left, right, far, counts, sums, back, own,
    a2a_send, a2a_recv, more_send, more_recv, hop_send, hop_recv, far_send, far_recv,
    cnt_send, cnt_recv, ret_send, ret_recv, early_send, early_recv, ready,
):
    me = lax.axis_index("freq")
    owner = lax.axis_index("pair")

    there = {by: jnp.logical_and(owner + by >= 0, owner + by < OWN) for by in (-2, -1, 1, 2)}
    inner = jnp.logical_and(there[-1], there[1])

    def along(by):
        return (me, lax.rem(owner + by + OWN, OWN))

    def signal(sem, device):
        pl.semaphore_signal(sem, 1, device_id=device, device_id_type=MESH)

    barrier = pltpu.get_barrier_semaphore()
    for by in (-1, 1):
        pl.when(there[by])(functools.partial(signal, barrier, along(by)))
    for by in range(1, FQ):
        signal(barrier, (lax.rem(me + by, FQ), owner))

    loads = [pltpu.make_async_copy(spec_hbm.at[:, w], spec.at[:, w], load_sem.at[w]) for w in range(W_DEV)]
    loads.append(pltpu.make_async_copy(blocks_hbm, blocks, load_sem.at[W_DEV]))
    loads.append(pltpu.make_async_copy(valid_hbm, valid, load_sem.at[W_DEV + 1]))
    for load in loads:
        load.start()
    loads[W_DEV].wait()
    loads[W_DEV + 1].wait()
    row = lax.broadcasted_iota(jnp.int32, (16, 16), 0)
    place = (blocks[0:1, :] - 2 * owner) * 8 + (blocks[1:2, :] - 2 * owner)
    table = jnp.sum(jnp.where(row == place, valid[...].astype(jnp.float32), 0.0), axis=1, keepdims=True)
    counts[2] = jnp.broadcast_to(table * (1.0 / (WIN * SB)), (16, SB))

    def copy(src, dst, send, recv, device):
        return pltpu.make_async_remote_copy(
            src_ref=src, dst_ref=dst, send_sem=send, recv_sem=recv, device_id=device, device_id_type=MESH
        )

    def shift(src, dst, send, recv, by):
        return Guarded(copy(src, dst, send, recv, along(by)), there[by], there[-by])

    def early(side, w):
        dst, by = ((from_right, -1), (from_left, 1))[side]
        return shift(
            white.at[:, w, :, pl.ds(0, F_PART), :], dst.at[:, w], early_send.at[side, w], early_recv.at[side, w], by
        )

    def early_relay(w):
        sent = copy(from_right.at[:, w], from_far.at[:, w], early_send.at[2, w], early_recv.at[2, w], along(-1))
        return Guarded(sent, inner, there[2])

    def regroup_more(i, by):
        peer = lax.rem(me + by, FQ)
        src = (from_left, from_right, from_far)[i]
        sent = copy(
            src.at[:, :, peer, :, :], more.at[i, by - 1],
            more_send.at[i, by - 1], more_recv.at[i, by - 1], (peer, owner),
        )
        held_here = there[(-1, 1, 2)[i]]
        return Guarded(sent, held_here, held_here)

    def part_bins(t):
        return pl.ds(pl.multiple_of(t * F_PART, F_PART), F_PART)

    def regroup(by, t):
        peer = lax.rem(me + by, FQ)
        return copy(
            white.at[:, :, peer, part_bins(t), :], landed.at[by - 1, :, :, part_bins(t), :],
            a2a_send.at[by - 1, t], a2a_recv.at[by - 1, t], (peer, owner),
        )

    def count_copies():
        return [
            shift(counts.at[2], counts.at[to], cnt_send.at[i], cnt_recv.at[i], by)
            for i, (to, by) in enumerate(((1, 1), (3, -1), (0, 2)))
        ]

    def hop(side, t, part):
        bins = pl.ds(t * F_PART + part * F_HALF, F_HALF)
        dst, by = ((right, -1), (left, 1))[side]
        at = 2 * t + part
        return shift(held.at[bins], dst.at[bins], hop_send.at[side, at], hop_recv.at[side, at], by)

    def relay(last, t, part):
        bins = pl.ds(t * F_PART + part * F_HALF, F_HALF)
        src, by = ((right, -1), (left, 1))[last]
        at = 2 * t + part
        sent = copy(src.at[bins], far.at[bins], far_send.at[at], far_recv.at[at], along(by))
        return Guarded(sent, inner, there[(2, -2)[last]])

    def returned(last, at, stage):
        bins = pl.ds(pl.multiple_of(at * F_HALF, F_HALF), F_HALF)
        plan = ((((2, 1, 1),), ((0, -1, 0), (3, 2, 2))), (((1, -1, 0),), ((3, 1, 1), (0, -2, 2))))[last][stage]
        return [
            shift(sums.at[slot, bins, :], back.at[to, bins, :], ret_send.at[to, at], ret_recv.at[to, at], by)
            for slot, by, to in plan
        ]

    def place_part(dst, t, first, others, arrived):
        for by in range(FQ):
            if by:
                arrived(by)
            for c in range(2):
                for w in range(W_DEV):
                    k = c * WIN + by * W_DEV + w
                    value = (others(by, c, w) if by else first(c, w)).astype(jnp.float32)
                    for h in range(2):
                        wide[h, k * F_PART : (k + 1) * F_PART, :] = value[:, h * SB : (h + 1) * SB]
        for f in range(F_PART):
            for h in range(2):
                value = wide[h, pl.ds(f, KDIM, stride=F_PART), :]
                dst[t * F_PART + f, :, h * SB : (h + 1) * SB] = value.astype(jnp.bfloat16)

    def arrange(t):
        bins = part_bins(t)
        place_part(
            held, t, lambda c, w: white[c, w, me, bins, :], lambda by, c, w: landed[by - 1, c, w, bins, :],
            lambda by: regroup(by, t).wait_recv(),
        )

    def arrange_more(i):
        src = (from_left, from_right, from_far)[i]

        @pl.when(there[(-1, 1, 2)[i]])
        def _():
            place_part(
                (left, right, far)[i], 0, lambda c, w: src[c, w, me], lambda by, c, w: more[i, by - 1, c, w],
                lambda by: regroup_more(i, by).copy.wait_recv(),
            )

    def clear(ref, first_bin, bins):
        @pl.loop(first_bin, first_bin + bins)
        def _(f):
            ref[f] = jnp.zeros(ref.shape[1:], ref.dtype)

    def clear_units(ref, last):
        for at in range(2 * T):
            if LAST[at] == last:
                clear(ref, at * F_HALF, F_HALF)

    def clear_missing():
        for by, near, back_at, count_at in ((-1, left, 1, 1), (1, right, 0, 3)):

            @pl.when(jnp.logical_not(there[by]))
            def _(near=near, back_at=back_at, count_at=count_at):
                clear(near, 0, F_DEV)
                back[back_at] = jnp.zeros((F_DEV, ST), jnp.float32)
                counts[count_at] = jnp.zeros((16, SB), jnp.float32)

        for by, last in ((-2, 1), (2, 0)):

            @pl.when(jnp.logical_not(there[by]))
            def _(last=last):
                clear_units(far, last)
                for at in range(2 * T):
                    if LAST[at] != last:
                        back[2, at * F_HALF : (at + 1) * F_HALF] = jnp.zeros((F_HALF, ST), jnp.float32)

        @pl.when(jnp.logical_not(there[-2]))
        def _():
            counts[0] = jnp.zeros((16, SB), jnp.float32)

    def compute_own(last):
        def weight(p, q):
            return counts[2, p * 8 + q : p * 8 + q + 1, :]

        for run in ((2, 4), (5, 6), (7, 8)) if last else ((0, 2), (4, 5), (6, 7)):

            @pl.loop(*run)
            def _(at):
                eight_bins(0, held, {0: held}, weight, pl.multiple_of(at * F_HALF, F_HALF), own)

    def start_hops(t):
        for side, part in ((0, 0), (1, 1), (0, 1), (1, 0)):
            hop(side, t, part).start()

    def pass_on(t):
        hop(0, t, 0).wait_recv()
        relay(0, t, 0).start()
        hop(1, t, 1).wait_recv()
        relay(1, t, 1).start()

    def weight_first(p, q):
        return counts[1, p * 8 + q : p * 8 + q + 1, :]

    def weight_last(p, q):
        at = (q % 2) * 8 + 6 - 2 * (q // 2) + p
        return counts[q // 2, at : at + 1, :]

    def compute(last, at, stage):
        start = pl.multiple_of(at * F_HALF, F_HALF)
        if last:
            partners = {0: far} if stage else {1: left, 2: held, 3: right}
            eight_bins(3, right, partners, weight_last, start, sums)
        else:
            partners = {3: far} if stage else {0: left, 1: held, 2: right}
            eight_bins(0, left, partners, weight_first, start, sums)
        for item in returned(last, at, stage):
            item.start()

    for w in range(W_DEV):
        loads[w].wait()
        whiten(spec, white, w, 1)
        if w == 0:
            pl.semaphore_wait(barrier, FQ - 1 + there[-1].astype(jnp.int32) + there[1].astype(jnp.int32))

            @pl.when(inner)
            def _():
                signal(ready.at[0], along(1))
                signal(ready.at[1], along(-1))

        early(0, w).start()
        early(1, w).start()
    for t in (1, 2, 3, 0):
        for by in range(1, FQ):
            regroup(by, t).start()
    for item in count_copies()[:2]:
        item.start()
    arrange(1)
    start_hops(1)
    for w in range(W_DEV):
        early(0, w).wait_recv()
        early(1, w).wait_recv()
    for i in range(2):
        for by in range(1, FQ):
            regroup_more(i, by).start()
    for i, by in ((0, -2), (1, 2)):

        @pl.when(there[by])
        def _(i=i):
            pl.semaphore_wait(ready.at[i], 1)

    count_copies()[2].start()

    @pl.loop(2, T)
    def _(t):
        arrange(t)
        start_hops(t)

    for w in range(W_DEV):
        early_relay(w).start()
    for part in range(2):
        hop(1, 1, part).wait_recv()
        relay(1, 1, part).start()
    clear_missing()
    for item in count_copies():
        item.wait_recv()
    hop(0, 1, 0).wait_recv()
    hop(0, 1, 1).wait_recv()

    @pl.loop(2, 4)
    def _(at):
        compute(1, at, 0)

    arrange(0)
    arrange_more(0)
    arrange_more(1)

    @pl.loop(0, 2)
    def _(at):
        compute(0, at, 0)

    @pl.loop(2, T)
    def _(t):
        pass_on(t)
        hop(1, t, 0).wait_recv()
        hop(0, t, 1).wait_recv()
        compute(0, 2 * t, 0)
        compute(1, 2 * t + 1, 0)

    for by, last in ((-1, 1), (1, 0)):

        @pl.when(jnp.logical_not(there[by]))
        def _(last=last):
            own[...] = jnp.zeros((1, F_DEV, ST), jnp.float32)
            compute_own(last)

    for w in range(W_DEV):
        early_relay(w).wait_recv()
    for by in range(1, FQ):
        regroup_more(2, by).start()

    @pl.loop(2, 4)
    def _(at):
        relay(1, 1, at - 2).wait_recv()
        compute(1, at, 1)

    @pl.loop(2, T)
    def _(t):
        relay(0, t, 0).wait_recv()
        compute(0, 2 * t, 1)
        relay(1, t, 1).wait_recv()
        compute(1, 2 * t + 1, 1)

        @pl.when(t == 2)
        def _():
            arrange_more(2)

            @pl.loop(0, 2)
            def _(at):
                compute(0, at, 1)

    for at in range(2 * T):
        last = LAST[at]
        for item in returned(last, at, 0) + returned(last, at, 1):
            item.wait_recv()
        bins = slice(at * F_HALF, (at + 1) * F_HALF)
        out[bins] = (sums[1 + last, bins] + back[0, bins]) + (back[1, bins] + back[2, bins])

    @pl.when(jnp.logical_not(inner))
    def _():
        out[...] += own[0]

    for t in range(T):
        for by in range(1, FQ):
            regroup(by, t).wait_send()
        for part in range(2):
            at = 2 * t + part
            last = LAST[at]
            if t:
                hop(0, t, part).wait_send()
                hop(1, t, part).wait_send()
                relay(last, t, part).wait_send()
            for item in returned(last, at, 0) + returned(last, at, 1):
                item.wait_send()
    for w in range(W_DEV):
        early(0, w).wait_send()
        early(1, w).wait_send()
        early_relay(w).wait_send()
    for i in range(3):
        for by in range(1, FQ):
            regroup_more(i, by).wait_send()
    for item in count_copies():
        item.wait_send()


def body(spectra, pair_blocks, pair_valid):
    dma = pltpu.SemaphoreType.DMA
    band = pltpu.VMEM((F_DEV, KDIM, ST), jnp.bfloat16)
    early = pltpu.VMEM((2, W_DEV, FQ, F_PART, ST), jnp.bfloat16)
    vmem = pl.BlockSpec(memory_space=pltpu.VMEM)
    anywhere = pl.BlockSpec(memory_space=pl.ANY)
    return pl.pallas_call(
        kernel,
        out_shape=jax.ShapeDtypeStruct((F_DEV, ST), jnp.float32),
        in_specs=[anywhere, anywhere, anywhere],
        out_specs=vmem,
        scratch_shapes=[
            pltpu.VMEM((2, W_DEV, FREQ, ST), jnp.bfloat16),
            pltpu.VMEM((2, 16), jnp.int32),
            pltpu.VMEM((1, 16), jnp.int32),
            dma((W_DEV + 2,)),
            pltpu.VMEM((2, W_DEV, FQ, F_DEV, ST), jnp.bfloat16),
            early, early, early,
            pltpu.VMEM((FQ - 1, 2, W_DEV, F_DEV, ST), jnp.bfloat16),
            pltpu.VMEM((3, FQ - 1, 2, W_DEV, F_PART, ST), jnp.bfloat16),
            pltpu.VMEM((2, KDIM * F_PART, SB), jnp.float32),
            band, band, band, band,
            pltpu.VMEM((4, 16, SB), jnp.float32),
            pltpu.VMEM((4, F_DEV, ST), jnp.float32),
            pltpu.VMEM((3, F_DEV, ST), jnp.float32),
            pltpu.VMEM((1, F_DEV, ST), jnp.float32),
            dma((FQ - 1, T)), dma((FQ - 1, T)),
            dma((3, FQ - 1)), dma((3, FQ - 1)),
            dma((2, 2 * T)), dma((2, 2 * T)),
            dma((2 * T,)), dma((2 * T,)),
            dma((3,)), dma((3,)),
            dma((3, 2 * T)), dma((3, 2 * T)),
            dma((3, W_DEV)), dma((3, W_DEV)),
            pltpu.SemaphoreType.REGULAR((2,)),
        ],
        compiler_params=pltpu.CompilerParams(
            collective_id=0, has_side_effects=True, vmem_limit_bytes=60 * 2**20
        ),
        cost_estimate=pl.CostEstimate(flops=8 * 10**9, bytes_accessed=2 * 2**20, transcendentals=0),
    )(spectra, pair_blocks.T, pair_valid.reshape(1, 16))


def solution(mesh):
    in_specs = (P(None, "freq", None, "pair"), P("pair", None), P("pair"))
    out_specs = P("freq", "pair")
    return jax.shard_map(body, mesh=mesh, in_specs=in_specs, out_specs=out_specs, check_vma=False)
```

```python
import functools

import jax
import jax.numpy as jnp
from jax import lax
from jax.experimental import pallas as pl
from jax.experimental.pallas import tpu as pltpu
from jax.sharding import PartitionSpec as P

MESH = pl.DeviceIdType.MESH
SB = 128
HALF = 64
EPS = 1e-06
TINY = 1.1754944e-38
FQ = 8
OWN = 64
WIN = 24
W_DEV = 3
FREQ = 512
F_DEV = 64
ST = 256
T = 4
F_PART = F_DEV // T
F_HALF = F_PART // 2
KDIM = 2 * WIN
UNROLL = 4
LAST = (0, 0, 1, 1, 0, 1, 0, 1)


def modulus(square):
    return square * lax.rsqrt(jnp.maximum(square, TINY))


def whiten(spec, white, first_window, windows):
    @pl.loop(first_window, first_window + windows)
    def _(w):
        re = spec[0, w].astype(jnp.float32)
        im = spec[1, w].astype(jnp.float32)
        mag = modulus(re * re + im * im)
        high = mag.astype(jnp.bfloat16)
        rest = mag - high.astype(jnp.float32)
        mid = rest.astype(jnp.bfloat16)
        low = (rest - mid.astype(jnp.float32)).astype(jnp.bfloat16)
        for tile in range(FREQ // 128):
            first = tile * 128
            start = min(max(first - HALF, 0), FREQ - 256)
            out_bin = lax.broadcasted_iota(jnp.int32, (128, 256), 0) + first
            in_bin = lax.broadcasted_iota(jnp.int32, (128, 256), 1) + start
            band = jnp.where(jnp.abs(out_bin - in_bin) <= HALF, 1.0, 0.0).astype(jnp.bfloat16)
            rows = slice(start, start + 256)
            total = jnp.dot(band, low[rows], preferred_element_type=jnp.float32)
            total += jnp.dot(band, mid[rows], preferred_element_type=jnp.float32)
            total += jnp.dot(band, high[rows], preferred_element_type=jnp.float32)
            bins = lax.broadcasted_iota(jnp.int32, (128, ST), 0) + first
            counted = jnp.minimum(bins + HALF, FREQ - 1) - jnp.maximum(bins - HALF, 0) + 1
            inverse = 1.0 / (total / counted.astype(jnp.float32) + EPS)
            here = slice(first, first + 128)
            two = slice(first // F_DEV, first // F_DEV + 2)
            white[0, w, two] = (re[here] * inverse).astype(jnp.bfloat16).reshape(2, F_DEV, ST)
            white[1, w, two] = (im[here] * inverse).astype(jnp.bfloat16).reshape(2, F_DEV, ST)


def one_bin(anchor, partners, weight, f):
    first = anchor[f]
    wide = first.astype(jnp.float32)
    turned = jnp.concatenate([wide[WIN:], -wide[:WIN]], axis=0).astype(jnp.bfloat16)
    left = jnp.concatenate([first, turned], axis=1).T
    right = {s: partner[f] for s, partner in partners.items()}
    cols = {}
    rows = []
    for p in range(2):
        pieces = []
        for i in range(2):
            at = p * SB + i * 64
            lhs = jnp.concatenate([left[at : at + 64], left[ST + at : ST + at + 64]], axis=0)
            piece = None
            for s in partners:
                cross = jnp.dot(lhs, right[s], preferred_element_type=jnp.float32)
                for h in range(2):
                    q = 2 * s + h
                    if not p <= q <= p + 6:
                        continue
                    lanes = slice(h * SB, (h + 1) * SB)
                    re, im = cross[:64, lanes], cross[64:, lanes]
                    value = modulus(re * re + im * im) * weight(p, q)
                    col = jnp.sum(value.reshape(8, 8, SB), axis=0)
                    cols[q] = cols[q] + col if q in cols else col
                    piece = value if piece is None else piece + value
            pieces.append(piece)
        across = jnp.concatenate(pieces, axis=0).T
        rows.append(jnp.sum(across.reshape(16, 8, SB), axis=0).sum(axis=0, keepdims=True))
    return rows, {q: col.sum(axis=0, keepdims=True) for q, col in cols.items()}


def eight_bins(units, out, waits=None):
    line = lax.broadcasted_iota(jnp.int32, (8, SB), 0)
    keys = []
    for anchor_slot, anchor, partners, weight, start in units:
        own = [2 * anchor_slot, 2 * anchor_slot + 1]
        keys.append(sorted({2 * s + h for s in partners for h in range(2)} | set(own)))

    def step(k, tiles):
        result = []
        for (anchor_slot, anchor, partners, weight, start), mine, old in zip(units, keys, tiles):
            rows, cols = one_bin(anchor, partners, weight, start + k)
            for p in range(2):
                q = 2 * anchor_slot + p
                cols[q] = cols[q] + rows[p] if anchor_slot in partners else rows[p]
            result.append(tuple(jnp.where(line == k, cols[q], tile) for q, tile in zip(mine, old)))
        return tuple(result)

    zero = jnp.zeros((8, SB), jnp.float32)
    tiles = tuple((zero,) * len(mine) for mine in keys)
    if waits:
        for half, wait in enumerate(waits):
            wait()
            tiles = lax.fori_loop(4 * half, 4 * half + 4, step, tiles, unroll=4)
    else:
        tiles = lax.fori_loop(0, 8, step, tiles, unroll=UNROLL if len(units[0][2]) > 1 else 8)
    for (anchor_slot, anchor, partners, weight, start), mine, new in zip(units, keys, tiles):
        for q, tile in zip(mine, new):
            place = (q // 2, pl.ds(start, 8), slice((q % 2) * SB, (q % 2 + 1) * SB))
            met = anchor_slot not in partners and q // 2 == anchor_slot
            out[place] = out[place] + tile if met else tile


class Guarded:
    def __init__(self, copy, sends, receives):
        self.copy, self.sends, self.receives = copy, sends, receives

    def start(self):
        @pl.when(self.sends)
        def _():
            self.copy.start()

    def wait_send(self):
        @pl.when(self.sends)
        def _():
            self.copy.wait_send()

    def wait_recv(self):
        @pl.when(self.receives)
        def _():
            self.copy.wait_recv()


def kernel(
    spec_hbm, blocks_hbm, valid_hbm, out,
    spec, blocks, valid, load_sem, white, from_left, from_right, from_far, landed, more, wide,
    held, left, right, far, counts, sums, back, own,
    a2a_send, a2a_recv, more_send, more_recv, hop_send, hop_recv, far_send, far_recv,
    cnt_send, cnt_recv, ret_send, ret_recv, early_send, early_recv, ready,
):
    me = lax.axis_index("freq")
    owner = lax.axis_index("pair")

    there = {by: jnp.logical_and(owner + by >= 0, owner + by < OWN) for by in (-2, -1, 1, 2)}
    inner = jnp.logical_and(there[-1], there[1])

    def along(by):
        return (me, lax.rem(owner + by + OWN, OWN))

    def signal(sem, device):
        pl.semaphore_signal(sem, 1, device_id=device, device_id_type=MESH)

    barrier = pltpu.get_barrier_semaphore()
    for by in (-1, 1):
        pl.when(there[by])(functools.partial(signal, barrier, along(by)))
    for by in range(1, FQ):
        signal(barrier, (lax.rem(me + by, FQ), owner))

    loads = [pltpu.make_async_copy(spec_hbm.at[:, w], spec.at[:, w], load_sem.at[w]) for w in range(W_DEV)]
    loads.append(pltpu.make_async_copy(blocks_hbm, blocks, load_sem.at[W_DEV]))
    loads.append(pltpu.make_async_copy(valid_hbm, valid, load_sem.at[W_DEV + 1]))
    for load in loads:
        load.start()
    loads[W_DEV].wait()
    loads[W_DEV + 1].wait()
    row = lax.broadcasted_iota(jnp.int32, (16, 16), 0)
    place = (blocks[0:1, :] - 2 * owner) * 8 + (blocks[1:2, :] - 2 * owner)
    table = jnp.sum(jnp.where(row == place, valid[...].astype(jnp.float32), 0.0), axis=1, keepdims=True)
    counts[2] = jnp.broadcast_to(table * (1.0 / (WIN * SB)), (16, SB))

    def copy(src, dst, send, recv, device):
        return pltpu.make_async_remote_copy(
            src_ref=src, dst_ref=dst, send_sem=send, recv_sem=recv, device_id=device, device_id_type=MESH
        )

    def shift(src, dst, send, recv, by):
        return Guarded(copy(src, dst, send, recv, along(by)), there[by], there[-by])

    def early(side, w):
        dst, by = ((from_right, -1), (from_left, 1))[side]
        return shift(
            white.at[:, w, :, pl.ds(0, F_PART), :], dst.at[:, w], early_send.at[side], early_recv.at[side, w], by
        )

    def early_relay(w):
        sent = copy(from_right.at[:, w], from_far.at[:, w], early_send.at[2], early_recv.at[2, w], along(-1))
        return Guarded(sent, inner, there[2])

    def regroup_more(i, by):
        peer = lax.rem(me + by, FQ)
        src = (from_left, from_right, from_far)[i]
        sent = copy(
            src.at[:, :, peer, :, :], more.at[i, by - 1],
            more_send.at[i], more_recv.at[i], (peer, owner),
        )
        held_here = there[(-1, 1, 2)[i]]
        return Guarded(sent, held_here, held_here)

    def regroup_more_all(i):
        held_here = there[(-1, 1, 2)[i]]
        return Guarded(copy(more.at[i], more.at[i], more_send.at[i], more_recv.at[i], (me, owner)), held_here, held_here)

    def part_bins(t):
        return pl.ds(pl.multiple_of(t * F_PART, F_PART), F_PART)

    def regroup(by, t):
        peer = lax.rem(me + by, FQ)
        return copy(
            white.at[:, :, peer, part_bins(t), :], landed.at[by - 1, :, :, part_bins(t), :],
            a2a_send.at[0], a2a_recv.at[t], (peer, owner),
        )

    def regroup_all(t):
        bins = landed.at[:, :, :, part_bins(t), :]
        return copy(bins, bins, a2a_send.at[0], a2a_recv.at[t], (me, owner))

    def count_copies():
        return [
            shift(counts.at[2], counts.at[to], cnt_send.at[i], cnt_recv.at[i], by)
            for i, (to, by) in enumerate(((1, 1), (3, -1), (0, 2)))
        ]

    def hop(side, t, part):
        bins = pl.ds(t * F_PART + part * F_HALF, F_HALF)
        dst, by = ((right, -1), (left, 1))[side]
        at = 2 * t + part - 2
        return shift(held.at[bins], dst.at[bins], hop_send.at[side], hop_recv.at[side, at], by)

    def relay(last, t, part, half):
        bins = pl.ds(t * F_PART + part * F_HALF + half * (F_HALF // 2), F_HALF // 2)
        src, by = ((right, -1), (left, 1))[last]
        at = 4 * t + 2 * part + half - 4
        sent = copy(src.at[bins], far.at[bins], far_send.at[0], far_recv.at[at], along(by))
        return Guarded(sent, inner, there[(2, -2)[last]])

    def returned(last, at, stage):
        bins = pl.ds(pl.multiple_of(at * F_HALF, F_HALF), F_HALF)
        plan = ((((2, 1, 1),), ((0, -1, 0), (3, 2, 2))), (((1, -1, 0),), ((3, 1, 1), (0, -2, 2))))[last][stage]
        items = []
        for slot, by, to in plan:
            sem = to + last if to == 2 else to
            items.append(shift(sums.at[slot, bins, :], back.at[to, bins, :], ret_send.at[sem], ret_recv.at[sem], by))
        return items

    def returned_all():
        half = F_DEV // 2
        return [
            shift(back.at[to, pl.ds(0, n), :], back.at[to, pl.ds(0, n), :], ret_send.at[i], ret_recv.at[i], by)
            for i, (to, n, by) in enumerate(((0, F_DEV, -1), (1, F_DEV, 1), (2, half, 2), (2, half, -2)))
        ]

    def place_part(dst, t, first, others):
        for by in range(FQ):
            for c in range(2):
                for w in range(W_DEV):
                    k = c * WIN + by * W_DEV + w
                    value = (others(by, c, w) if by else first(c, w)).astype(jnp.float32)
                    for h in range(2):
                        wide[h, k * F_PART : (k + 1) * F_PART, :] = value[:, h * SB : (h + 1) * SB]
        for f in range(F_PART):
            for h in range(2):
                value = wide[h, pl.ds(f, KDIM, stride=F_PART), :]
                dst[t * F_PART + f, :, h * SB : (h + 1) * SB] = value.astype(jnp.bfloat16)

    def arrange(t):
        bins = part_bins(t)
        regroup_all(t).wait_recv()
        place_part(
            held, t, lambda c, w: white[c, w, me, bins, :], lambda by, c, w: landed[by - 1, c, w, bins, :]
        )

    def arrange_more(i):
        src = (from_left, from_right, from_far)[i]

        @pl.when(there[(-1, 1, 2)[i]])
        def _():
            regroup_more_all(i).copy.wait_recv()
            place_part((left, right, far)[i], 0, lambda c, w: src[c, w, me], lambda by, c, w: more[i, by - 1, c, w])

    def clear(ref, first_bin, bins):
        @pl.loop(first_bin, first_bin + bins)
        def _(f):
            ref[f] = jnp.zeros(ref.shape[1:], ref.dtype)

    def clear_units(ref, last):
        for at in range(2 * T):
            if LAST[at] == last:
                clear(ref, at * F_HALF, F_HALF)

    def clear_missing():
        for by, near, back_at, count_at in ((-1, left, 1, 1), (1, right, 0, 3)):

            @pl.when(jnp.logical_not(there[by]))
            def _(near=near, back_at=back_at, count_at=count_at):
                clear(near, 0, F_DEV)
                back[back_at] = jnp.zeros((F_DEV, ST), jnp.float32)
                counts[count_at] = jnp.zeros((16, SB), jnp.float32)

        for by, last in ((-2, 1), (2, 0)):

            @pl.when(jnp.logical_not(there[by]))
            def _(last=last):
                clear_units(far, last)
                for at in range(2 * T):
                    if LAST[at] != last:
                        back[2, at * F_HALF : (at + 1) * F_HALF] = jnp.zeros((F_HALF, ST), jnp.float32)

        @pl.when(jnp.logical_not(there[-2]))
        def _():
            counts[0] = jnp.zeros((16, SB), jnp.float32)

    def compute_own(last):
        def weight(p, q):
            return counts[2, p * 8 + q : p * 8 + q + 1, :]

        for run in ((2, 4), (5, 6), (7, 8)) if last else ((0, 2), (4, 5), (6, 7)):

            @pl.loop(*run)
            def _(at):
                eight_bins([(0, held, {0: held}, weight, pl.multiple_of(at * F_HALF, F_HALF))], own)

    def start_hops(t):
        for side, part in ((0, 0), (1, 1), (0, 1), (1, 0)):
            hop(side, t, part).start()

    def pass_on(t):
        hop(0, t, 0).wait_recv()
        hop(1, t, 1).wait_recv()
        for half in range(2):
            relay(0, t, 0, half).start()
            relay(1, t, 1, half).start()

    def weight_first(p, q):
        return counts[1, p * 8 + q : p * 8 + q + 1, :]

    def weight_last(p, q):
        at = (q % 2) * 8 + 6 - 2 * (q // 2) + p
        return counts[q // 2, at : at + 1, :]

    def unit(last, at, stage):
        start = pl.multiple_of(at * F_HALF, F_HALF)
        if last:
            return (3, right, {0: far} if stage else {1: left, 2: held, 3: right}, weight_last, start)
        return (0, left, {3: far} if stage else {0: left, 1: held, 2: right}, weight_first, start)

    def compute(last, at, stage):
        eight_bins([unit(last, at, stage)], sums)
        for item in returned(last, at, stage):
            item.start()

    def compute_far(t):
        def wait(half):
            relay(0, t, 0, half).wait_recv()
            relay(1, t, 1, half).wait_recv()

        eight_bins([unit(0, 2 * t, 1), unit(1, 2 * t + 1, 1)], sums, [functools.partial(wait, half) for half in range(2)])
        for item in returned(0, 2 * t, 1) + returned(1, 2 * t + 1, 1):
            item.start()

    for w in range(W_DEV):
        loads[w].wait()
        whiten(spec, white, w, 1)
        if w == 0:
            pl.semaphore_wait(barrier, FQ - 1 + there[-1].astype(jnp.int32) + there[1].astype(jnp.int32))

            @pl.when(inner)
            def _():
                signal(ready.at[0], along(1))
                signal(ready.at[1], along(-1))

        early(0, w).start()
        early(1, w).start()
    for t in (1, 2, 3, 0):
        for by in range(1, FQ):
            regroup(by, t).start()
    for item in count_copies()[:2]:
        item.start()
    arrange(1)
    start_hops(1)
    for w in range(W_DEV):
        early(0, w).wait_recv()
        early(1, w).wait_recv()
    for i in range(2):
        for by in range(1, FQ):
            regroup_more(i, by).start()
    for i, by in ((0, -2), (1, 2)):

        @pl.when(there[by])
        def _(i=i):
            pl.semaphore_wait(ready.at[i], 1)

    count_copies()[2].start()

    @pl.loop(2, T)
    def _(t):
        arrange(t)
        start_hops(t)

    for w in range(W_DEV):
        early_relay(w).start()
    for part in range(2):
        hop(1, 1, part).wait_recv()
        for half in range(2):
            relay(1, 1, part, half).start()
    clear_missing()
    for item in count_copies():
        item.wait_recv()
    hop(0, 1, 0).wait_recv()
    hop(0, 1, 1).wait_recv()

    @pl.loop(2, 4)
    def _(at):
        compute(1, at, 0)

    arrange(0)
    arrange_more(0)
    arrange_more(1)

    @pl.loop(0, 2)
    def _(at):
        compute(0, at, 0)

    @pl.loop(2, T)
    def _(t):
        pass_on(t)
        hop(1, t, 0).wait_recv()
        hop(0, t, 1).wait_recv()
        compute(0, 2 * t, 0)
        compute(1, 2 * t + 1, 0)

    for by, last in ((-1, 1), (1, 0)):

        @pl.when(jnp.logical_not(there[by]))
        def _(last=last):
            own[...] = jnp.zeros((1, F_DEV, ST), jnp.float32)
            compute_own(last)

    for w in range(W_DEV):
        early_relay(w).wait_recv()
    for by in range(1, FQ):
        regroup_more(2, by).start()

    @pl.loop(2, 4)
    def _(at):
        for half in range(2):
            relay(1, 1, at - 2, half).wait_recv()
        compute(1, at, 1)

    @pl.loop(2, T)
    def _(t):
        compute_far(t)

        @pl.when(t == 2)
        def _():
            arrange_more(2)

            @pl.loop(0, 2)
            def _(at):
                compute(0, at, 1)

    for item in returned_all():
        item.wait_recv()
    for at in range(2 * T):
        bins = slice(at * F_HALF, (at + 1) * F_HALF)
        out[bins] = (sums[1 + LAST[at], bins] + back[0, bins]) + (back[1, bins] + back[2, bins])

    @pl.when(jnp.logical_not(inner))
    def _():
        out[...] += own[0]

    copy(landed, landed, a2a_send.at[0], a2a_recv.at[0], (me, owner)).wait_send()
    rest = pl.ds(F_PART, F_DEV - F_PART)
    for side, by in ((0, -1), (1, 1)):
        shift(held.at[rest], held.at[rest], hop_send.at[side], hop_recv.at[side, 0], by).wait_send()
        shift(from_left, from_left, early_send.at[side], early_recv.at[side, 0], by).wait_send()
    Guarded(copy(from_far, from_far, early_send.at[2], early_recv.at[2, 0], along(-1)), inner, inner).wait_send()
    Guarded(copy(held.at[rest], far.at[rest], far_send.at[0], far_recv.at[0], along(-1)), inner, inner).wait_send()
    for i in range(3):
        regroup_more_all(i).wait_send()
    for item in returned_all() + count_copies():
        item.wait_send()


def body(spectra, pair_blocks, pair_valid):
    dma = pltpu.SemaphoreType.DMA
    band = pltpu.VMEM((F_DEV, KDIM, ST), jnp.bfloat16)
    early = pltpu.VMEM((2, W_DEV, FQ, F_PART, ST), jnp.bfloat16)
    vmem = pl.BlockSpec(memory_space=pltpu.VMEM)
    anywhere = pl.BlockSpec(memory_space=pl.ANY)
    return pl.pallas_call(
        kernel,
        out_shape=jax.ShapeDtypeStruct((F_DEV, ST), jnp.float32),
        in_specs=[anywhere, anywhere, anywhere],
        out_specs=vmem,
        scratch_shapes=[
            pltpu.VMEM((2, W_DEV, FREQ, ST), jnp.bfloat16),
            pltpu.VMEM((2, 16), jnp.int32),
            pltpu.VMEM((1, 16), jnp.int32),
            dma((W_DEV + 2,)),
            pltpu.VMEM((2, W_DEV, FQ, F_DEV, ST), jnp.bfloat16),
            early, early, early,
            pltpu.VMEM((FQ - 1, 2, W_DEV, F_DEV, ST), jnp.bfloat16),
            pltpu.VMEM((3, FQ - 1, 2, W_DEV, F_PART, ST), jnp.bfloat16),
            pltpu.VMEM((2, KDIM * F_PART, SB), jnp.float32),
            band, band, band, band,
            pltpu.VMEM((4, 16, SB), jnp.float32),
            pltpu.VMEM((4, F_DEV, ST), jnp.float32),
            pltpu.VMEM((3, F_DEV, ST), jnp.float32),
            pltpu.VMEM((1, F_DEV, ST), jnp.float32),
            dma((1,)), dma((T,)),
            dma((3,)), dma((3,)),
            dma((2,)), dma((2, 2 * T - 2)),
            dma((1,)), dma((4 * T - 4,)),
            dma((3,)), dma((3,)),
            dma((4,)), dma((4,)),
            dma((3,)), dma((3, W_DEV)),
            pltpu.SemaphoreType.REGULAR((2,)),
        ],
        compiler_params=pltpu.CompilerParams(
            collective_id=0, has_side_effects=True, vmem_limit_bytes=60 * 2**20
        ),
        cost_estimate=pl.CostEstimate(flops=8 * 10**9, bytes_accessed=2 * 2**20, transcendentals=0),
    )(spectra, pair_blocks.T, pair_valid.reshape(1, 16))


def solution(mesh):
    in_specs = (P(None, "freq", None, "pair"), P("pair", None), P("pair"))
    out_specs = P("freq", "pair")
    return jax.shard_map(body, mesh=mesh, in_specs=in_specs, out_specs=out_specs, check_vma=False)
```

```python
import functools

import jax
import jax.numpy as jnp
from jax import lax
from jax.experimental import pallas as pl
from jax.experimental.pallas import tpu as pltpu
from jax.sharding import PartitionSpec as P

MESH = pl.DeviceIdType.MESH
SB = 128
HALF = 64
EPS = 1e-06
TINY = 1.1754944e-38
FQ = 8
OWN = 64
WIN = 24
W_DEV = 3
FREQ = 512
F_DEV = 64
ST = 256
T = 4
F_PART = F_DEV // T
F_HALF = F_PART // 2
KDIM = 2 * WIN
UNROLL = 4
LAST = (0, 0, 1, 1, 0, 1, 0, 1)


def modulus(square):
    return square * lax.rsqrt(jnp.maximum(square, TINY))


def whiten(spec, white, first_window, windows):
    @pl.loop(first_window, first_window + windows)
    def _(w):
        re = spec[0, w].astype(jnp.float32)
        im = spec[1, w].astype(jnp.float32)
        mag = modulus(re * re + im * im)
        high = mag.astype(jnp.bfloat16)
        rest = mag - high.astype(jnp.float32)
        mid = rest.astype(jnp.bfloat16)
        low = (rest - mid.astype(jnp.float32)).astype(jnp.bfloat16)
        for tile in range(FREQ // 128):
            first = tile * 128
            start = min(max(first - HALF, 0), FREQ - 256)
            out_bin = lax.broadcasted_iota(jnp.int32, (128, 256), 0) + first
            in_bin = lax.broadcasted_iota(jnp.int32, (128, 256), 1) + start
            band = jnp.where(jnp.abs(out_bin - in_bin) <= HALF, 1.0, 0.0).astype(jnp.bfloat16)
            rows = slice(start, start + 256)
            total = jnp.dot(band, low[rows], preferred_element_type=jnp.float32)
            total += jnp.dot(band, mid[rows], preferred_element_type=jnp.float32)
            total += jnp.dot(band, high[rows], preferred_element_type=jnp.float32)
            bins = lax.broadcasted_iota(jnp.int32, (128, ST), 0) + first
            counted = jnp.minimum(bins + HALF, FREQ - 1) - jnp.maximum(bins - HALF, 0) + 1
            inverse = 1.0 / (total / counted.astype(jnp.float32) + EPS)
            here = slice(first, first + 128)
            two = slice(first // F_DEV, first // F_DEV + 2)
            white[0, w, two] = (re[here] * inverse).astype(jnp.bfloat16).reshape(2, F_DEV, ST)
            white[1, w, two] = (im[here] * inverse).astype(jnp.bfloat16).reshape(2, F_DEV, ST)


def one_bin(anchor, partners, weight, f):
    first = anchor[f]
    wide = first.astype(jnp.float32)
    turned = jnp.concatenate([wide[WIN:], -wide[:WIN]], axis=0).astype(jnp.bfloat16)
    left = jnp.concatenate([first, turned], axis=1).T
    right = {s: partner[f] for s, partner in partners.items()}
    cols = {}
    rows = []
    for p in range(2):
        pieces = []
        for i in range(2):
            at = p * SB + i * 64
            lhs = jnp.concatenate([left[at : at + 64], left[ST + at : ST + at + 64]], axis=0)
            piece = None
            for s in partners:
                cross = jnp.dot(lhs, right[s], preferred_element_type=jnp.float32)
                for h in range(2):
                    q = 2 * s + h
                    if not p <= q <= p + 6:
                        continue
                    lanes = slice(h * SB, (h + 1) * SB)
                    re, im = cross[:64, lanes], cross[64:, lanes]
                    value = modulus(re * re + im * im) * weight(p, q)
                    col = jnp.sum(value.reshape(8, 8, SB), axis=0)
                    cols[q] = cols[q] + col if q in cols else col
                    piece = value if piece is None else piece + value
            pieces.append(piece)
        across = jnp.concatenate(pieces, axis=0).T
        rows.append(jnp.sum(across.reshape(16, 8, SB), axis=0).sum(axis=0, keepdims=True))
    return rows, {q: col.sum(axis=0, keepdims=True) for q, col in cols.items()}


def eight_bins(units, out, waits=None):
    line = lax.broadcasted_iota(jnp.int32, (8, SB), 0)
    keys = []
    for anchor_slot, anchor, partners, weight, start in units:
        own = [2 * anchor_slot, 2 * anchor_slot + 1]
        keys.append(sorted({2 * s + h for s in partners for h in range(2)} | set(own)))

    def step(k, tiles):
        result = []
        for (anchor_slot, anchor, partners, weight, start), mine, old in zip(units, keys, tiles):
            rows, cols = one_bin(anchor, partners, weight, start + k)
            for p in range(2):
                q = 2 * anchor_slot + p
                cols[q] = cols[q] + rows[p] if anchor_slot in partners else rows[p]
            result.append(tuple(jnp.where(line == k, cols[q], tile) for q, tile in zip(mine, old)))
        return tuple(result)

    zero = jnp.zeros((8, SB), jnp.float32)
    tiles = tuple((zero,) * len(mine) for mine in keys)
    if waits:
        for half, wait in enumerate(waits):
            wait()
            tiles = lax.fori_loop(4 * half, 4 * half + 4, step, tiles, unroll=4)
    else:
        tiles = lax.fori_loop(0, 8, step, tiles, unroll=UNROLL if len(units[0][2]) > 1 else 8)
    for (anchor_slot, anchor, partners, weight, start), mine, new in zip(units, keys, tiles):
        for q, tile in zip(mine, new):
            place = (q // 2, pl.ds(start, 8), slice((q % 2) * SB, (q % 2 + 1) * SB))
            met = anchor_slot not in partners and q // 2 == anchor_slot
            out[place] = out[place] + tile if met else tile


class Guarded:
    def __init__(self, copy, sends, receives):
        self.copy, self.sends, self.receives = copy, sends, receives

    def start(self):
        @pl.when(self.sends)
        def _():
            self.copy.start()

    def wait_send(self):
        @pl.when(self.sends)
        def _():
            self.copy.wait_send()

    def wait_recv(self):
        @pl.when(self.receives)
        def _():
            self.copy.wait_recv()


def kernel(
    spec_hbm, slots, out,
    spec, load_sem, white, from_left, from_right, from_far, landed, more, wide,
    held, left, right, far, counts, sums, back, own,
    a2a_send, a2a_recv, more_send, more_recv, hop_send, hop_recv, far_send, far_recv,
    cnt_send, cnt_recv, ret_send, ret_recv, early_send, early_recv, ready,
):
    me = lax.axis_index("freq")
    owner = lax.axis_index("pair")

    there = {by: jnp.logical_and(owner + by >= 0, owner + by < OWN) for by in (-2, -1, 1, 2)}
    inner = jnp.logical_and(there[-1], there[1])

    def along(by):
        return (me, lax.rem(owner + by + OWN, OWN))

    def signal(sem, device):
        pl.semaphore_signal(sem, 1, device_id=device, device_id_type=MESH)

    barrier = pltpu.get_barrier_semaphore()
    for by in (-1, 1):
        pl.when(there[by])(functools.partial(signal, barrier, along(by)))
    for by in range(1, FQ):
        signal(barrier, (lax.rem(me + by, FQ), owner))

    loads = [pltpu.make_async_copy(spec_hbm.at[:, w], spec.at[:, w], load_sem.at[w]) for w in range(W_DEV)]
    for load in loads:
        load.start()
    row = lax.broadcasted_iota(jnp.int32, (16, 16), 0)
    place = slots[...] - 18 * owner
    table = jnp.sum(jnp.where(row == place, 1.0, 0.0), axis=1, keepdims=True)
    counts[2] = jnp.broadcast_to(table * (1.0 / (WIN * SB)), (16, SB))

    def copy(src, dst, send, recv, device):
        return pltpu.make_async_remote_copy(
            src_ref=src, dst_ref=dst, send_sem=send, recv_sem=recv, device_id=device, device_id_type=MESH
        )

    def shift(src, dst, send, recv, by):
        return Guarded(copy(src, dst, send, recv, along(by)), there[by], there[-by])

    def early(side, w):
        dst, by = ((from_right, -1), (from_left, 1))[side]
        return shift(
            white.at[:, w, :, pl.ds(0, F_PART), :], dst.at[:, w], early_send.at[side], early_recv.at[side], by
        )

    def early_relay(w):
        sent = copy(from_right.at[:, w], from_far.at[:, w], early_send.at[2], early_recv.at[2], along(-1))
        return Guarded(sent, inner, there[2])

    def regroup_more(i, by):
        peer = lax.rem(me + by, FQ)
        src = (from_left, from_right, from_far)[i]
        sent = copy(
            src.at[:, :, peer, :, :], more.at[i, by - 1],
            more_send.at[i], more_recv.at[i], (peer, owner),
        )
        held_here = there[(-1, 1, 2)[i]]
        return Guarded(sent, held_here, held_here)

    def regroup_more_all(i):
        held_here = there[(-1, 1, 2)[i]]
        return Guarded(copy(more.at[i], more.at[i], more_send.at[i], more_recv.at[i], (me, owner)), held_here, held_here)

    def part_bins(t):
        return pl.ds(pl.multiple_of(t * F_PART, F_PART), F_PART)

    def regroup(by, t):
        peer = lax.rem(me + by, FQ)
        return copy(
            white.at[:, :, peer, part_bins(t), :], landed.at[by - 1, :, :, part_bins(t), :],
            a2a_send.at[0], a2a_recv.at[t], (peer, owner),
        )

    def regroup_all(t):
        bins = landed.at[:, :, :, part_bins(t), :]
        return copy(bins, bins, a2a_send.at[0], a2a_recv.at[t], (me, owner))

    def count_copies():
        return [
            shift(counts.at[2], counts.at[to], cnt_send.at[i], cnt_recv.at[i], by)
            for i, (to, by) in enumerate(((1, 1), (3, -1), (0, 2)))
        ]

    def hop(side, t, part):
        bins = pl.ds(t * F_PART + part * F_HALF, F_HALF)
        dst, by = ((right, -1), (left, 1))[side]
        at = 2 * t + part - 2
        return shift(held.at[bins], dst.at[bins], hop_send.at[side], hop_recv.at[side, at], by)

    def relay(last, t, part, half):
        bins = pl.ds(t * F_PART + part * F_HALF + half * (F_HALF // 2), F_HALF // 2)
        src, by = ((right, -1), (left, 1))[last]
        at = 4 * t + 2 * part + half - 4
        sent = copy(src.at[bins], far.at[bins], far_send.at[0], far_recv.at[at], along(by))
        return Guarded(sent, inner, there[(2, -2)[last]])

    def returned(last, at, stage):
        bins = pl.ds(pl.multiple_of(at * F_HALF, F_HALF), F_HALF)
        plan = ((((2, 1, 1),), ((0, -1, 0), (3, 2, 2))), (((1, -1, 0),), ((3, 1, 1), (0, -2, 2))))[last][stage]
        items = []
        for slot, by, to in plan:
            sem = to + last if to == 2 else to
            items.append(shift(sums.at[slot, bins, :], back.at[to, bins, :], ret_send.at[sem], ret_recv.at[sem], by))
        return items

    def returned_all():
        half = F_DEV // 2
        return [
            shift(back.at[to, pl.ds(0, n), :], back.at[to, pl.ds(0, n), :], ret_send.at[i], ret_recv.at[i], by)
            for i, (to, n, by) in enumerate(((0, F_DEV, -1), (1, F_DEV, 1), (2, half, 2), (2, half, -2)))
        ]

    def place_part(dst, t, first, others):
        for by in range(FQ):
            for c in range(2):
                for w in range(W_DEV):
                    k = c * WIN + by * W_DEV + w
                    value = (others(by, c, w) if by else first(c, w)).astype(jnp.float32)
                    for h in range(2):
                        wide[h, k * F_PART : (k + 1) * F_PART, :] = value[:, h * SB : (h + 1) * SB]
        for f in range(F_PART):
            for h in range(2):
                value = wide[h, pl.ds(f, KDIM, stride=F_PART), :]
                dst[t * F_PART + f, :, h * SB : (h + 1) * SB] = value.astype(jnp.bfloat16)

    def arrange(t):
        bins = part_bins(t)
        regroup_all(t).wait_recv()
        place_part(
            held, t, lambda c, w: white[c, w, me, bins, :], lambda by, c, w: landed[by - 1, c, w, bins, :]
        )

    def arrange_more(i):
        src = (from_left, from_right, from_far)[i]

        @pl.when(there[(-1, 1, 2)[i]])
        def _():
            regroup_more_all(i).copy.wait_recv()
            place_part((left, right, far)[i], 0, lambda c, w: src[c, w, me], lambda by, c, w: more[i, by - 1, c, w])

    def clear(ref, first_bin, bins):
        @pl.loop(first_bin, first_bin + bins)
        def _(f):
            ref[f] = jnp.zeros(ref.shape[1:], ref.dtype)

    def clear_units(ref, last):
        for at in range(2 * T):
            if LAST[at] == last:
                clear(ref, at * F_HALF, F_HALF)

    def clear_missing():
        for by, near, back_at, count_at in ((-1, left, 1, 1), (1, right, 0, 3)):

            @pl.when(jnp.logical_not(there[by]))
            def _(near=near, back_at=back_at, count_at=count_at):
                clear(near, 0, F_DEV)
                back[back_at] = jnp.zeros((F_DEV, ST), jnp.float32)
                counts[count_at] = jnp.zeros((16, SB), jnp.float32)

        for by, last in ((-2, 1), (2, 0)):

            @pl.when(jnp.logical_not(there[by]))
            def _(last=last):
                clear_units(far, last)
                for at in range(2 * T):
                    if LAST[at] != last:
                        back[2, at * F_HALF : (at + 1) * F_HALF] = jnp.zeros((F_HALF, ST), jnp.float32)

        @pl.when(jnp.logical_not(there[-2]))
        def _():
            counts[0] = jnp.zeros((16, SB), jnp.float32)

    def compute_own(last):
        def weight(p, q):
            return counts[2, p * 8 + q : p * 8 + q + 1, :]

        for run in ((2, 4), (5, 6), (7, 8)) if last else ((0, 2), (4, 5), (6, 7)):

            @pl.loop(*run)
            def _(at):
                eight_bins([(0, held, {0: held}, weight, pl.multiple_of(at * F_HALF, F_HALF))], own)

    def start_hops(t):
        for side, part in ((0, 0), (1, 1), (0, 1), (1, 0)):
            hop(side, t, part).start()

    def pass_on(t):
        hop(0, t, 0).wait_recv()
        hop(1, t, 1).wait_recv()
        for half in range(2):
            relay(0, t, 0, half).start()
            relay(1, t, 1, half).start()

    def weight_first(p, q):
        return counts[1, p * 8 + q : p * 8 + q + 1, :]

    def weight_last(p, q):
        at = (q % 2) * 8 + 6 - 2 * (q // 2) + p
        return counts[q // 2, at : at + 1, :]

    def unit(last, at, stage):
        start = pl.multiple_of(at * F_HALF, F_HALF)
        if last:
            return (3, right, {0: far} if stage else {1: left, 2: held, 3: right}, weight_last, start)
        return (0, left, {3: far} if stage else {0: left, 1: held, 2: right}, weight_first, start)

    def compute(last, at, stage):
        eight_bins([unit(last, at, stage)], sums)
        for item in returned(last, at, stage):
            item.start()

    def compute_far(t):
        def wait(half):
            relay(0, t, 0, half).wait_recv()
            relay(1, t, 1, half).wait_recv()

        eight_bins([unit(0, 2 * t, 1), unit(1, 2 * t + 1, 1)], sums, [functools.partial(wait, half) for half in range(2)])
        for item in returned(0, 2 * t, 1) + returned(1, 2 * t + 1, 1):
            item.start()

    for w in range(W_DEV):
        loads[w].wait()
        whiten(spec, white, w, 1)
        if w == 0:
            pl.semaphore_wait(barrier, FQ - 1 + there[-1].astype(jnp.int32) + there[1].astype(jnp.int32))

            @pl.when(inner)
            def _():
                signal(ready.at[0], along(1))
                signal(ready.at[1], along(-1))

        early(0, w).start()
        early(1, w).start()
    for t in (1, 2, 3, 0):
        for by in range(1, FQ):
            regroup(by, t).start()
    for item in count_copies()[:2]:
        item.start()
    arrange(1)
    start_hops(1)
    for side, by in ((0, -1), (1, 1)):
        shift(from_left, from_left, early_send.at[side], early_recv.at[side], by).wait_recv()
    for i in range(2):
        for by in range(1, FQ):
            regroup_more(i, by).start()
    for i, by in ((0, -2), (1, 2)):

        @pl.when(there[by])
        def _(i=i):
            pl.semaphore_wait(ready.at[i], 1)

    count_copies()[2].start()

    @pl.loop(2, T)
    def _(t):
        arrange(t)
        start_hops(t)

    for w in range(W_DEV):
        early_relay(w).start()
    for part in range(2):
        hop(1, 1, part).wait_recv()
        for half in range(2):
            relay(1, 1, part, half).start()
    clear_missing()
    for item in count_copies():
        item.wait_recv()
    hop(0, 1, 0).wait_recv()
    hop(0, 1, 1).wait_recv()

    @pl.loop(2, 4)
    def _(at):
        compute(1, at, 0)

    arrange(0)
    arrange_more(0)
    arrange_more(1)

    @pl.loop(0, 2)
    def _(at):
        compute(0, at, 0)

    @pl.loop(2, T)
    def _(t):
        pass_on(t)
        hop(1, t, 0).wait_recv()
        hop(0, t, 1).wait_recv()
        compute(0, 2 * t, 0)
        compute(1, 2 * t + 1, 0)

    for by, last in ((-1, 1), (1, 0)):

        @pl.when(jnp.logical_not(there[by]))
        def _(last=last):
            own[...] = jnp.zeros((1, F_DEV, ST), jnp.float32)
            compute_own(last)

    Guarded(copy(from_far, from_far, early_send.at[2], early_recv.at[2], along(-1)), there[2], there[2]).wait_recv()
    for by in range(1, FQ):
        regroup_more(2, by).start()

    @pl.loop(2, 4)
    def _(at):
        for half in range(2):
            relay(1, 1, at - 2, half).wait_recv()
        compute(1, at, 1)

    @pl.loop(2, T)
    def _(t):
        compute_far(t)

        @pl.when(t == 2)
        def _():
            arrange_more(2)

            @pl.loop(0, 2)
            def _(at):
                compute(0, at, 1)

    copy(landed, landed, a2a_send.at[0], a2a_recv.at[0], (me, owner)).wait_send()
    rest = pl.ds(F_PART, F_DEV - F_PART)
    for side, by in ((0, -1), (1, 1)):
        shift(held.at[rest], held.at[rest], hop_send.at[side], hop_recv.at[side, 0], by).wait_send()
        shift(from_left, from_left, early_send.at[side], early_recv.at[side], by).wait_send()
    Guarded(copy(from_far, from_far, early_send.at[2], early_recv.at[2], along(-1)), inner, inner).wait_send()
    Guarded(copy(held.at[rest], far.at[rest], far_send.at[0], far_recv.at[0], along(-1)), inner, inner).wait_send()
    for i in range(3):
        regroup_more_all(i).wait_send()
    for item in count_copies():
        item.wait_send()
    for item in returned_all():
        item.wait_recv()
    for at in range(2 * T):
        bins = slice(at * F_HALF, (at + 1) * F_HALF)
        out[bins] = (sums[1 + LAST[at], bins] + back[0, bins]) + (back[1, bins] + back[2, bins])

    @pl.when(jnp.logical_not(inner))
    def _():
        out[...] += own[0]

    for item in returned_all():
        item.wait_send()


def body(spectra, pair_blocks, pair_valid):
    dma = pltpu.SemaphoreType.DMA
    slots = jnp.where(pair_valid == 1, pair_blocks[:, 0] * 8 + pair_blocks[:, 1], -1).reshape(1, 16)
    band = pltpu.VMEM((F_DEV, KDIM, ST), jnp.bfloat16)
    early = pltpu.VMEM((2, W_DEV, FQ, F_PART, ST), jnp.bfloat16)
    vmem = pl.BlockSpec(memory_space=pltpu.VMEM)
    anywhere = pl.BlockSpec(memory_space=pl.ANY)
    return pl.pallas_call(
        kernel,
        out_shape=jax.ShapeDtypeStruct((F_DEV, ST), jnp.float32),
        in_specs=[anywhere, vmem],
        out_specs=vmem,
        scratch_shapes=[
            pltpu.VMEM((2, W_DEV, FREQ, ST), jnp.bfloat16),
            dma((W_DEV,)),
            pltpu.VMEM((2, W_DEV, FQ, F_DEV, ST), jnp.bfloat16),
            early, early, early,
            pltpu.VMEM((FQ - 1, 2, W_DEV, F_DEV, ST), jnp.bfloat16),
            pltpu.VMEM((3, FQ - 1, 2, W_DEV, F_PART, ST), jnp.bfloat16),
            pltpu.VMEM((2, KDIM * F_PART, SB), jnp.float32),
            band, band, band, band,
            pltpu.VMEM((4, 16, SB), jnp.float32),
            pltpu.VMEM((4, F_DEV, ST), jnp.float32),
            pltpu.VMEM((3, F_DEV, ST), jnp.float32),
            pltpu.VMEM((1, F_DEV, ST), jnp.float32),
            dma((1,)), dma((T,)),
            dma((3,)), dma((3,)),
            dma((2,)), dma((2, 2 * T - 2)),
            dma((1,)), dma((4 * T - 4,)),
            dma((3,)), dma((3,)),
            dma((4,)), dma((4,)),
            dma((3,)), dma((3,)),
            pltpu.SemaphoreType.REGULAR((2,)),
        ],
        compiler_params=pltpu.CompilerParams(
            collective_id=0, has_side_effects=True, vmem_limit_bytes=53 * 2**20
        ),
        cost_estimate=pl.CostEstimate(flops=8 * 10**9, bytes_accessed=2 * 2**20, transcendentals=0),
    )(spectra, slots)


def solution(mesh):
    in_specs = (P(None, "freq", None, "pair"), P("pair", None), P("pair"))
    out_specs = P("freq", "pair")
    return jax.shard_map(body, mesh=mesh, in_specs=in_specs, out_specs=out_specs, check_vma=False)
```

```python
import functools

import jax
import jax.numpy as jnp
from jax import lax
from jax.experimental import pallas as pl
from jax.experimental.pallas import tpu as pltpu
from jax.sharding import PartitionSpec as P

MESH = pl.DeviceIdType.MESH
SB = 128
HALF = 64
EPS = 1e-06
TINY = 1.1754944e-38
FQ = 8
OWN = 64
WIN = 24
W_DEV = 3
FREQ = 512
F_DEV = 64
ST = 256
T = 4
F_PART = F_DEV // T
F_HALF = F_PART // 2
KDIM = 2 * WIN
UNROLL = 4
PIECES = ((0, 6), (6, 8))
LAST = (0, 0, 1, 1, 0, 1, 0, 1)


def modulus(square):
    return square * lax.rsqrt(jnp.maximum(square, TINY))


def whiten(spec, white, first_window, windows):
    @pl.loop(first_window, first_window + windows)
    def _(w):
        re = spec[0, w].astype(jnp.float32)
        im = spec[1, w].astype(jnp.float32)
        mag = modulus(re * re + im * im)
        high = mag.astype(jnp.bfloat16)
        rest = mag - high.astype(jnp.float32)
        mid = rest.astype(jnp.bfloat16)
        low = (rest - mid.astype(jnp.float32)).astype(jnp.bfloat16)
        for tile in range(FREQ // 128):
            first = tile * 128
            start = min(max(first - HALF, 0), FREQ - 256)
            out_bin = lax.broadcasted_iota(jnp.int32, (128, 256), 0) + first
            in_bin = lax.broadcasted_iota(jnp.int32, (128, 256), 1) + start
            band = jnp.where(jnp.abs(out_bin - in_bin) <= HALF, 1.0, 0.0).astype(jnp.bfloat16)
            rows = slice(start, start + 256)
            total = jnp.dot(band, low[rows], preferred_element_type=jnp.float32)
            total += jnp.dot(band, mid[rows], preferred_element_type=jnp.float32)
            total += jnp.dot(band, high[rows], preferred_element_type=jnp.float32)
            bins = lax.broadcasted_iota(jnp.int32, (128, ST), 0) + first
            counted = jnp.minimum(bins + HALF, FREQ - 1) - jnp.maximum(bins - HALF, 0) + 1
            inverse = 1.0 / (total / counted.astype(jnp.float32) + EPS)
            here = slice(first, first + 128)
            two = slice(first // F_DEV, first // F_DEV + 2)
            white[0, w, two] = (re[here] * inverse).astype(jnp.bfloat16).reshape(2, F_DEV, ST)
            white[1, w, two] = (im[here] * inverse).astype(jnp.bfloat16).reshape(2, F_DEV, ST)


def one_bin(anchor, partners, weight, f):
    first = anchor[f]
    wide = first.astype(jnp.float32)
    turned = jnp.concatenate([wide[WIN:], -wide[:WIN]], axis=0).astype(jnp.bfloat16)
    left = jnp.concatenate([first, turned], axis=1).T
    right = {s: partner[f] for s, partner in partners.items()}
    cols = {}
    rows = []
    for p in range(2):
        pieces = []
        for i in range(2):
            at = p * SB + i * 64
            lhs = jnp.concatenate([left[at : at + 64], left[ST + at : ST + at + 64]], axis=0)
            piece = None
            for s in partners:
                cross = jnp.dot(lhs, right[s], preferred_element_type=jnp.float32)
                for h in range(2):
                    q = 2 * s + h
                    if not p <= q <= p + 6:
                        continue
                    lanes = slice(h * SB, (h + 1) * SB)
                    re, im = cross[:64, lanes], cross[64:, lanes]
                    value = modulus(re * re + im * im) * weight(p, q)
                    col = jnp.sum(value.reshape(8, 8, SB), axis=0)
                    cols[q] = cols[q] + col if q in cols else col
                    piece = value if piece is None else piece + value
            pieces.append(piece)
        across = jnp.concatenate(pieces, axis=0).T
        rows.append(jnp.sum(across.reshape(16, 8, SB), axis=0).sum(axis=0, keepdims=True))
    return rows, {q: col.sum(axis=0, keepdims=True) for q, col in cols.items()}


def eight_bins(units, out, waits=None):
    line = lax.broadcasted_iota(jnp.int32, (8, SB), 0)
    keys = []
    for anchor_slot, anchor, partners, weight, start in units:
        own = [2 * anchor_slot, 2 * anchor_slot + 1]
        keys.append(sorted({2 * s + h for s in partners for h in range(2)} | set(own)))

    def step(k, tiles):
        result = []
        for (anchor_slot, anchor, partners, weight, start), mine, old in zip(units, keys, tiles):
            rows, cols = one_bin(anchor, partners, weight, start + k)
            for p in range(2):
                q = 2 * anchor_slot + p
                cols[q] = cols[q] + rows[p] if anchor_slot in partners else rows[p]
            result.append(tuple(jnp.where(line == k, cols[q], tile) for q, tile in zip(mine, old)))
        return tuple(result)

    zero = jnp.zeros((8, SB), jnp.float32)
    tiles = tuple((zero,) * len(mine) for mine in keys)
    if waits:
        for half, wait in enumerate(waits):
            wait()
            first, end = PIECES[half]
            tiles = lax.fori_loop(first, end, step, tiles, unroll=end - first)
    else:
        tiles = lax.fori_loop(0, 8, step, tiles, unroll=UNROLL if len(units[0][2]) > 1 else 8)
    for (anchor_slot, anchor, partners, weight, start), mine, new in zip(units, keys, tiles):
        for q, tile in zip(mine, new):
            place = (q // 2, pl.ds(start, 8), slice((q % 2) * SB, (q % 2 + 1) * SB))
            met = anchor_slot not in partners and q // 2 == anchor_slot
            out[place] = out[place] + tile if met else tile


class Guarded:
    def __init__(self, copy, sends, receives):
        self.copy, self.sends, self.receives = copy, sends, receives

    def start(self):
        @pl.when(self.sends)
        def _():
            self.copy.start()

    def wait_send(self):
        @pl.when(self.sends)
        def _():
            self.copy.wait_send()

    def wait_recv(self):
        @pl.when(self.receives)
        def _():
            self.copy.wait_recv()


def kernel(
    spec_hbm, slots, out,
    spec, load_sem, white, from_left, from_right, from_far, landed, more, wide,
    held, left, right, far, counts, sums, back, own,
    a2a_send, a2a_recv, more_send, more_recv, hop_send, hop_recv, far_send, far_recv,
    cnt_send, cnt_recv, ret_send, ret_recv, early_send, early_recv, ready,
):
    me = lax.axis_index("freq")
    owner = lax.axis_index("pair")

    there = {by: jnp.logical_and(owner + by >= 0, owner + by < OWN) for by in (-2, -1, 1, 2)}
    inner = jnp.logical_and(there[-1], there[1])

    def along(by):
        return (me, lax.rem(owner + by + OWN, OWN))

    def signal(sem, device):
        pl.semaphore_signal(sem, 1, device_id=device, device_id_type=MESH)

    barrier = pltpu.get_barrier_semaphore()
    for by in (-1, 1):
        pl.when(there[by])(functools.partial(signal, barrier, along(by)))
    for by in range(1, FQ):
        signal(barrier, (lax.rem(me + by, FQ), owner))

    loads = [pltpu.make_async_copy(spec_hbm.at[:, w], spec.at[:, w], load_sem.at[w]) for w in range(W_DEV)]
    for load in loads:
        load.start()
    row = lax.broadcasted_iota(jnp.int32, (16, 16), 0)
    place = slots[...] - 18 * owner
    table = jnp.sum(jnp.where(row == place, 1.0, 0.0), axis=1, keepdims=True)
    counts[2] = jnp.broadcast_to(table * (1.0 / (WIN * SB)), (16, SB))

    def copy(src, dst, send, recv, device):
        return pltpu.make_async_remote_copy(
            src_ref=src, dst_ref=dst, send_sem=send, recv_sem=recv, device_id=device, device_id_type=MESH
        )

    def shift(src, dst, send, recv, by):
        return Guarded(copy(src, dst, send, recv, along(by)), there[by], there[-by])

    def early(side, w):
        dst, by = ((from_right, -1), (from_left, 1))[side]
        return shift(
            white.at[:, w, :, pl.ds(0, F_PART), :], dst.at[:, w], early_send.at[side], early_recv.at[side], by
        )

    def early_relay(w):
        sent = copy(from_right.at[:, w], from_far.at[:, w], early_send.at[2], early_recv.at[2], along(-1))
        return Guarded(sent, inner, there[2])

    def regroup_more(i, by):
        peer = lax.rem(me + by, FQ)
        src = (from_left, from_right, from_far)[i]
        sent = copy(
            src.at[:, :, peer, :, :], more.at[i, by - 1],
            more_send.at[i], more_recv.at[i], (peer, owner),
        )
        held_here = there[(-1, 1, 2)[i]]
        return Guarded(sent, held_here, held_here)

    def regroup_more_all(i):
        held_here = there[(-1, 1, 2)[i]]
        return Guarded(copy(more.at[i], more.at[i], more_send.at[i], more_recv.at[i], (me, owner)), held_here, held_here)

    def part_bins(t):
        return pl.ds(pl.multiple_of(t * F_PART, F_PART), F_PART)

    def regroup(by, t):
        peer = lax.rem(me + by, FQ)
        return copy(
            white.at[:, :, peer, part_bins(t), :], landed.at[by - 1, :, :, part_bins(t), :],
            a2a_send.at[0], a2a_recv.at[t], (peer, owner),
        )

    def regroup_all(t):
        bins = landed.at[:, :, :, part_bins(t), :]
        return copy(bins, bins, a2a_send.at[0], a2a_recv.at[t], (me, owner))

    def count_copies():
        return [
            shift(counts.at[2], counts.at[to], cnt_send.at[i], cnt_recv.at[i], by)
            for i, (to, by) in enumerate(((1, 1), (3, -1), (0, 2)))
        ]

    def hop(side, t, part):
        bins = pl.ds(t * F_PART + part * F_HALF, F_HALF)
        dst, by = ((right, -1), (left, 1))[side]
        at = 2 * t + part - 2
        return shift(held.at[bins], dst.at[bins], hop_send.at[side], hop_recv.at[side, at], by)

    def relay(last, t, part, half):
        bins = pl.ds(t * F_PART + part * F_HALF + PIECES[half][0], PIECES[half][1] - PIECES[half][0])
        src, by = ((right, -1), (left, 1))[last]
        at = 4 * t + 2 * part + half - 4
        sent = copy(src.at[bins], far.at[bins], far_send.at[0], far_recv.at[at], along(by))
        return Guarded(sent, inner, there[(2, -2)[last]])

    def returned(last, at, stage):
        bins = pl.ds(pl.multiple_of(at * F_HALF, F_HALF), F_HALF)
        plan = ((((2, 1, 1),), ((0, -1, 0), (3, 2, 2))), (((1, -1, 0),), ((3, 1, 1), (0, -2, 2))))[last][stage]
        items = []
        for slot, by, to in plan:
            sem = to + last if to == 2 else to
            items.append(shift(sums.at[slot, bins, :], back.at[to, bins, :], ret_send.at[sem], ret_recv.at[sem], by))
        return items

    def returned_all():
        half = F_DEV // 2
        return [
            shift(back.at[to, pl.ds(0, n), :], back.at[to, pl.ds(0, n), :], ret_send.at[i], ret_recv.at[i], by)
            for i, (to, n, by) in enumerate(((0, F_DEV, -1), (1, F_DEV, 1), (2, half, 2), (2, half, -2)))
        ]

    def place_part(dst, t, first, others):
        for by in range(FQ):
            for c in range(2):
                for w in range(W_DEV):
                    k = c * WIN + by * W_DEV + w
                    value = (others(by, c, w) if by else first(c, w)).astype(jnp.float32)
                    for h in range(2):
                        wide[h, k * F_PART : (k + 1) * F_PART, :] = value[:, h * SB : (h + 1) * SB]
        for f in range(F_PART):
            for h in range(2):
                value = wide[h, pl.ds(f, KDIM, stride=F_PART), :]
                dst[t * F_PART + f, :, h * SB : (h + 1) * SB] = value.astype(jnp.bfloat16)

    def arrange(t):
        bins = part_bins(t)
        regroup_all(t).wait_recv()
        place_part(
            held, t, lambda c, w: white[c, w, me, bins, :], lambda by, c, w: landed[by - 1, c, w, bins, :]
        )

    def arrange_more(i):
        src = (from_left, from_right, from_far)[i]

        @pl.when(there[(-1, 1, 2)[i]])
        def _():
            regroup_more_all(i).copy.wait_recv()
            place_part((left, right, far)[i], 0, lambda c, w: src[c, w, me], lambda by, c, w: more[i, by - 1, c, w])

    def clear(ref, first_bin, bins):
        @pl.loop(first_bin, first_bin + bins)
        def _(f):
            ref[f] = jnp.zeros(ref.shape[1:], ref.dtype)

    def clear_units(ref, last):
        for at in range(2 * T):
            if LAST[at] == last:
                clear(ref, at * F_HALF, F_HALF)

    def clear_missing():
        for by, near, back_at, count_at in ((-1, left, 1, 1), (1, right, 0, 3)):

            @pl.when(jnp.logical_not(there[by]))
            def _(near=near, back_at=back_at, count_at=count_at):
                clear(near, 0, F_DEV)
                back[back_at] = jnp.zeros((F_DEV, ST), jnp.float32)
                counts[count_at] = jnp.zeros((16, SB), jnp.float32)

        for by, last in ((-2, 1), (2, 0)):

            @pl.when(jnp.logical_not(there[by]))
            def _(last=last):
                clear_units(far, last)
                for at in range(2 * T):
                    if LAST[at] != last:
                        back[2, at * F_HALF : (at + 1) * F_HALF] = jnp.zeros((F_HALF, ST), jnp.float32)

        @pl.when(jnp.logical_not(there[-2]))
        def _():
            counts[0] = jnp.zeros((16, SB), jnp.float32)

    def compute_own(last):
        def weight(p, q):
            return counts[2, p * 8 + q : p * 8 + q + 1, :]

        for run in ((2, 4), (5, 6), (7, 8)) if last else ((0, 2), (4, 5), (6, 7)):

            @pl.loop(*run)
            def _(at):
                eight_bins([(0, held, {0: held}, weight, pl.multiple_of(at * F_HALF, F_HALF))], own)

    def start_hops(t):
        for side, part in ((0, 0), (1, 1), (0, 1), (1, 0)):
            hop(side, t, part).start()

    def pass_on(t):
        hop(0, t, 0).wait_recv()
        hop(1, t, 1).wait_recv()
        for half in range(2):
            relay(0, t, 0, half).start()
            relay(1, t, 1, half).start()

    def weight_first(p, q):
        return counts[1, p * 8 + q : p * 8 + q + 1, :]

    def weight_last(p, q):
        at = (q % 2) * 8 + 6 - 2 * (q // 2) + p
        return counts[q // 2, at : at + 1, :]

    def unit(last, at, stage):
        start = pl.multiple_of(at * F_HALF, F_HALF)
        if last:
            return (3, right, {0: far} if stage else {1: left, 2: held, 3: right}, weight_last, start)
        return (0, left, {3: far} if stage else {0: left, 1: held, 2: right}, weight_first, start)

    def compute(last, at, stage):
        eight_bins([unit(last, at, stage)], sums)
        for item in returned(last, at, stage):
            item.start()

    def compute_far(t):
        def wait(half):
            relay(0, t, 0, half).wait_recv()
            relay(1, t, 1, half).wait_recv()

        eight_bins([unit(0, 2 * t, 1), unit(1, 2 * t + 1, 1)], sums, [functools.partial(wait, half) for half in range(2)])
        for item in returned(0, 2 * t, 1) + returned(1, 2 * t + 1, 1):
            item.start()

    for w in range(W_DEV):
        loads[w].wait()
        whiten(spec, white, w, 1)
        if w == 0:
            pl.semaphore_wait(barrier, FQ - 1 + there[-1].astype(jnp.int32) + there[1].astype(jnp.int32))

            @pl.when(inner)
            def _():
                signal(ready.at[0], along(1))
                signal(ready.at[1], along(-1))

        early(0, w).start()
        early(1, w).start()
    for t in (1, 2, 3, 0):
        for by in range(1, FQ):
            regroup(by, t).start()
    for item in count_copies()[:2]:
        item.start()
    arrange(1)
    start_hops(1)
    for side, by in ((0, -1), (1, 1)):
        shift(from_left, from_left, early_send.at[side], early_recv.at[side], by).wait_recv()
    for i in range(2):
        for by in range(1, FQ):
            regroup_more(i, by).start()
    for i, by in ((0, -2), (1, 2)):

        @pl.when(there[by])
        def _(i=i):
            pl.semaphore_wait(ready.at[i], 1)

    count_copies()[2].start()

    @pl.loop(2, T)
    def _(t):
        arrange(t)
        start_hops(t)

    for w in range(W_DEV):
        early_relay(w).start()
    for part in range(2):
        hop(1, 1, part).wait_recv()
        for half in range(2):
            relay(1, 1, part, half).start()
    clear_missing()
    for item in count_copies():
        item.wait_recv()
    hop(0, 1, 0).wait_recv()
    hop(0, 1, 1).wait_recv()

    @pl.loop(2, 4)
    def _(at):
        compute(1, at, 0)

    arrange(0)
    arrange_more(0)
    arrange_more(1)

    @pl.loop(0, 2)
    def _(at):
        compute(0, at, 0)

    @pl.loop(2, T)
    def _(t):
        pass_on(t)
        hop(1, t, 0).wait_recv()
        hop(0, t, 1).wait_recv()
        compute(0, 2 * t, 0)
        compute(1, 2 * t + 1, 0)

    for by, last in ((-1, 1), (1, 0)):

        @pl.when(jnp.logical_not(there[by]))
        def _(last=last):
            own[...] = jnp.zeros((1, F_DEV, ST), jnp.float32)
            compute_own(last)

    Guarded(copy(from_far, from_far, early_send.at[2], early_recv.at[2], along(-1)), there[2], there[2]).wait_recv()
    for by in range(1, FQ):
        regroup_more(2, by).start()

    @pl.loop(2, 4)
    def _(at):
        for half in range(2):
            relay(1, 1, at - 2, half).wait_recv()
        compute(1, at, 1)

    @pl.loop(2, T)
    def _(t):
        compute_far(t)

        @pl.when(t == 2)
        def _():
            arrange_more(2)

            @pl.loop(0, 2)
            def _(at):
                compute(0, at, 1)

    copy(landed, landed, a2a_send.at[0], a2a_recv.at[0], (me, owner)).wait_send()
    rest = pl.ds(F_PART, F_DEV - F_PART)
    for side, by in ((0, -1), (1, 1)):
        shift(held.at[rest], held.at[rest], hop_send.at[side], hop_recv.at[side, 0], by).wait_send()
        shift(from_left, from_left, early_send.at[side], early_recv.at[side], by).wait_send()
    Guarded(copy(from_far, from_far, early_send.at[2], early_recv.at[2], along(-1)), inner, inner).wait_send()
    Guarded(copy(held.at[rest], far.at[rest], far_send.at[0], far_recv.at[0], along(-1)), inner, inner).wait_send()
    for i in range(3):
        regroup_more_all(i).wait_send()
    for item in count_copies():
        item.wait_send()
    for item in returned_all():
        item.wait_recv()
    for at in range(2 * T):
        bins = slice(at * F_HALF, (at + 1) * F_HALF)
        out[bins] = (sums[1 + LAST[at], bins] + back[0, bins]) + (back[1, bins] + back[2, bins])

    @pl.when(jnp.logical_not(inner))
    def _():
        out[...] += own[0]

    for item in returned_all():
        item.wait_send()


def body(spectra, pair_blocks, pair_valid):
    dma = pltpu.SemaphoreType.DMA
    slots = jnp.where(pair_valid == 1, pair_blocks[:, 0] * 8 + pair_blocks[:, 1], -1).reshape(1, 16)
    band = pltpu.VMEM((F_DEV, KDIM, ST), jnp.bfloat16)
    early = pltpu.VMEM((2, W_DEV, FQ, F_PART, ST), jnp.bfloat16)
    vmem = pl.BlockSpec(memory_space=pltpu.VMEM)
    anywhere = pl.BlockSpec(memory_space=pl.ANY)
    return pl.pallas_call(
        kernel,
        out_shape=jax.ShapeDtypeStruct((F_DEV, ST), jnp.float32),
        in_specs=[anywhere, vmem],
        out_specs=vmem,
        scratch_shapes=[
            pltpu.VMEM((2, W_DEV, FREQ, ST), jnp.bfloat16),
            dma((W_DEV,)),
            pltpu.VMEM((2, W_DEV, FQ, F_DEV, ST), jnp.bfloat16),
            early, early, early,
            pltpu.VMEM((FQ - 1, 2, W_DEV, F_DEV, ST), jnp.bfloat16),
            pltpu.VMEM((3, FQ - 1, 2, W_DEV, F_PART, ST), jnp.bfloat16),
            pltpu.VMEM((2, KDIM * F_PART, SB), jnp.float32),
            band, band, band, band,
            pltpu.VMEM((4, 16, SB), jnp.float32),
            pltpu.VMEM((4, F_DEV, ST), jnp.float32),
            pltpu.VMEM((3, F_DEV, ST), jnp.float32),
            pltpu.VMEM((1, F_DEV, ST), jnp.float32),
            dma((1,)), dma((T,)),
            dma((3,)), dma((3,)),
            dma((2,)), dma((2, 2 * T - 2)),
            dma((1,)), dma((4 * T - 4,)),
            dma((3,)), dma((3,)),
            dma((4,)), dma((4,)),
            dma((3,)), dma((3,)),
            pltpu.SemaphoreType.REGULAR((2,)),
        ],
        compiler_params=pltpu.CompilerParams(
            collective_id=0, has_side_effects=True, vmem_limit_bytes=53 * 2**20
        ),
        cost_estimate=pl.CostEstimate(flops=8 * 10**9, bytes_accessed=2 * 2**20, transcendentals=0),
    )(spectra, slots)


def solution(mesh):
    in_specs = (P(None, "freq", None, "pair"), P("pair", None), P("pair"))
    out_specs = P("freq", "pair")
    return jax.shard_map(body, mesh=mesh, in_specs=in_specs, out_specs=out_specs, check_vma=False)
```
